32 devices in a mesh: rep: 16 (over z, y, core), fsdp: 2 (over x).
Axes of the slice: x: 2, y: 2, z: 4, core: 2. Of those that a mesh axis runs over, the one named last changes fastest.
Arguments:
- tokens: bfloat16 [16384, 896], P(('rep', 'fsdp')), may hold values from -6 to 6
- segments: int32 [16384], P(('rep', 'fsdp')), may hold values from -1 to 3, as said below
- cotangent: bfloat16 [16384, 896], P(('rep', 'fsdp')), may hold values from -6 to 6
- w_query: bfloat16 [896, 896], P('fsdp'), may hold values from -0.1875 to 0.1875
- w_key: bfloat16 [896, 128], P('fsdp'), may hold values from -0.1875 to 0.1875
- w_value: bfloat16 [896, 128], P('fsdp'), may hold values from -0.1875 to 0.1875
- w_output: bfloat16 [896, 896], P('fsdp'), may hold values from -0.75 to 0.75
- w_gate: bfloat16 [896, 4864], P('fsdp'), may hold values from -0.1875 to 0.1875
- w_up: bfloat16 [896, 4864], P('fsdp'), may hold values from -0.1875 to 0.1875
- w_down: bfloat16 [4864, 896], P('fsdp'), may hold values from -0.078125 to 0.078125
- b_query: bfloat16 [896], P('fsdp'), may hold values from -2 to 2
- b_key: bfloat16 [128], P('fsdp'), may hold values from -2 to 2
- b_value: bfloat16 [128], P('fsdp'), may hold values from -2 to 2
- gain_attn: bfloat16 [896], P('fsdp'), may hold values from 0.5 to 1.5
- gain_mlp: bfloat16 [896], P('fsdp'), may hold values from 0.5 to 1.5
Outputs:
- output: bfloat16 [16384, 896], P(('rep', 'fsdp'))
- tokens_grad: float32 [16384, 896], P(('rep', 'fsdp'))
- w_query_grad: float32 [896, 896], P('fsdp')
- w_key_grad: float32 [896, 128], P('fsdp')
- w_value_grad: float32 [896, 128], P('fsdp')
- w_output_grad: float32 [896, 896], P('fsdp')
- w_gate_grad: float32 [896, 4864], P('fsdp')
- w_up_grad: float32 [896, 4864], P('fsdp')
- w_down_grad: float32 [4864, 896], P('fsdp')
- b_query_grad: float32 [896], P('fsdp')
- b_key_grad: float32 [128], P('fsdp')
- b_value_grad: float32 [128], P('fsdp')
- gain_attn_grad: float32 [896], P('fsdp')
- gain_mlp_grad: float32 [896], P('fsdp')
The draws below stay inside these ranges and needn't reach their ends.
Inputs may be any that keep to these rules, and one draw needn't show every extreme that they name: `segments`: in each device's 512 slots the used slots come first with segment numbers that never fall, the unused ones last; at least 128 slots of every device are used, and on one device all slots hold one sequence.
All inputs are finite; a program needn't handle non-finite values.
Results may differ from the reference program's by a relative error of at most 0.024.
Values may be sent and summed in bfloat16 or wider, within the bound.
No kernel may reach another device: no remote copies, remote signals or barrier semaphores. Data moves between devices by JAX's collectives and lax.ppermute only.
A program may use at most 256 MiB of HBM per device.

```python
import jax
import jax.numpy as jnp
from jax import lax

D = 896
HEADS = 14
KV_HEADS = 2
HEAD_DIM = 64
FF = 4864
TOK_DEV = 512
TOKENS = 16384
KVW = 128


def draw_segments(key, part):
    key = jax.random.fold_in(key, 11)
    key_lives, key_chosen, key_offsets = jax.random.split(key, 3)
    device_count = TOKENS // TOK_DEV
    used_rows = jax.random.randint(key_lives, (device_count,), TOK_DEV // 4, TOK_DEV)
    chosen = jax.random.randint(key_chosen, (), 0, device_count)
    single = jnp.arange(device_count) == chosen
    used_rows = jnp.where(single, TOK_DEV, used_rows)
    quarter = used_rows // 4
    spread = quarter // 3
    offsets = jax.random.randint(key_offsets, (device_count, 3), -spread[:, None], spread[:, None] + 1)
    borders = jnp.arange(1, 4, dtype=jnp.int32)[None, :] * quarter[:, None] + offsets
    borders = jnp.where(single[:, None], TOK_DEV, borders)
    slot_index = jnp.arange(TOK_DEV, dtype=jnp.int32)
    labels = jnp.sum((slot_index[None, :, None] >= borders[:, None, :]).astype(jnp.int32), axis=-1)
    labels = jnp.where(slot_index[None, :] < used_rows[:, None], labels, -1)
    return labels.reshape(TOKENS).astype(jnp.int32)


def level_of(own_key, dims, cuts, low, largest):
    factor_of = 1.0
    for axis_at, parts in cuts:
        steps = jax.random.uniform(jax.random.fold_in(jax.random.fold_in(own_key, 6), axis_at), (parts,), jnp.float32, low / len(cuts), largest / len(cuts))
        factor_of = factor_of * jnp.repeat(jnp.exp(steps), dims[axis_at] // parts).reshape((-1,) + (1,) * (len(dims) - 1 - axis_at))
    return factor_of


def noise(stream_key, shape, deviation, most, cuts=(), kind=jnp.bfloat16):
    level = level_of(stream_key, shape, cuts, -0.22, 0.18) if cuts else 1.0
    values = jax.random.normal(stream_key, shape, jnp.float32) * deviation * level
    return jnp.minimum(jnp.maximum(values, -most), most).astype(kind)


def setup_inputs(seed: int = 0) -> dict:
    streams_of = jax.random.split(jax.random.key(seed), 16)
    tokens = noise(streams_of[0], (TOKENS, D), 1.0, 6.0, ((0, 32),))
    segments = draw_segments(jax.random.fold_in(streams_of[15], 71), 0)
    cotangent = noise(streams_of[2], (TOKENS, D), 1.0, 6.0, ((0, 32),))
    w_query = noise(streams_of[3], (D, D), D ** -0.5, 0.1875, ((0, 2),))
    w_key = noise(streams_of[4], (D, KVW), D ** -0.5, 0.1875, ((0, 2),))
    w_value = noise(streams_of[5], (D, KVW), D ** -0.5, 0.1875, ((0, 2),))
    w_output = noise(streams_of[6], (D, D), (D // 16) ** -0.5, 0.75, ((0, 2),))
    w_gate = noise(streams_of[7], (D, FF), D ** -0.5, 0.1875, ((0, 2),))
    w_up = noise(streams_of[8], (D, FF), D ** -0.5, 0.1875, ((0, 2),))
    w_down = noise(streams_of[9], (FF, D), FF ** -0.5, 0.078125, ((0, 2),))
    b_query = noise(streams_of[10], (D,), 0.3, 2.0, ((0, 2),))
    b_key = noise(streams_of[11], (KVW,), 0.3, 2.0, ((0, 2),))
    b_value = noise(streams_of[12], (KVW,), 0.3, 2.0, ((0, 2),))
    gain_attn = jnp.clip(1.0 + 0.1 * jax.random.normal(streams_of[13], (D,), jnp.float32), 0.5, 1.5).astype(jnp.bfloat16)
    gain_mlp = jnp.clip(1.0 + 0.1 * jax.random.normal(streams_of[14], (D,), jnp.float32), 0.5, 1.5).astype(jnp.bfloat16)
    return dict(tokens=tokens, segments=segments, cotangent=cotangent, w_query=w_query, w_key=w_key, w_value=w_value, w_output=w_output, w_gate=w_gate, w_up=w_up, w_down=w_down, b_query=b_query, b_key=b_key, b_value=b_value, gain_attn=gain_attn, gain_mlp=gain_mlp)


EPSILON = 1e-06
THETA = 1000000.0
NEGATIVE = -1e+30
HIGH = lax.Precision.HIGHEST

@jax.custom_vjp
def low(v):
    return lax.optimization_barrier(v.astype(jnp.bfloat16)).astype(jnp.float32)

@jax.custom_vjp
def low_back(v):
    return v

def low_keep(v):
    return (low(v), None)

def low_pass(kept, grad):
    return (grad,)

def back_keep(v):
    return (v, None)

def back_low(kept, grad):
    return (low(grad),)
low.defvjp(low_keep, low_pass)
low_back.defvjp(back_keep, back_low)

def positions(segs):
    length = segs.shape[0]
    index = jnp.arange(length, dtype=jnp.int32)
    before = jnp.concatenate([jnp.full((1,), -2, dtype=jnp.int32), segs[:-1].astype(jnp.int32)])
    starts = lax.cummax(jnp.where(segs.astype(jnp.int32) != before, index, jnp.zeros_like(index)), axis=0)
    return (index - starts).astype(jnp.float32)

def rope_tables(segs, head_dim):
    halfway = head_dim // 2
    inverse = THETA ** (-(jnp.arange(halfway, dtype=jnp.float32) * 2.0 / head_dim))
    angles = positions(segs)[:, None] * inverse[None, :]
    return (jnp.cos(angles), jnp.sin(angles))

def rotate(values, cosine, sine):
    halfway = values.shape[-1] // 2
    first = values[..., :halfway]
    second = values[..., halfway:]
    cosine = cosine[:, None, :]
    sine = sine[:, None, :]
    return jnp.concatenate([first * cosine - second * sine, second * cosine + first * sine], axis=-1)

def normed(values, gain):
    scale = lax.rsqrt(lax.optimization_barrier(jnp.mean(values * values, axis=-1, keepdims=True)) + EPSILON)
    return values * scale * gain

def product(left, right):
    return jnp.dot(left, right, precision=HIGH)

def attend(queries, keys, values, segs):
    length = segs.shape[0]
    scale = queries.shape[-1] ** (-0.5)
    raw = low_back(jnp.einsum('tgd,sd->gts', queries, keys, precision=HIGH) * scale)
    index = jnp.arange(length, dtype=jnp.int32)
    allowed = (segs[:, None] == segs[None, :]) & (index[:, None] >= index[None, :])
    scores = jnp.where(allowed[None], raw, NEGATIVE)
    probs = low(jax.nn.softmax(scores, axis=-1))
    return jnp.einsum('gts,sd->tgd', probs, values, precision=HIGH)

def block_layer(hidden_in, segs, w_query, w_key, w_value, w_output, w_gate, w_up, w_down, b_query, b_key, b_value, gain_attn, gain_mlp):
    length = hidden_in.shape[0]
    groups = HEADS // KV_HEADS
    live = (segs >= 0).astype(hidden_in.dtype)[:, None]
    cosine, sine = rope_tables(segs, HEAD_DIM)
    normed_in = low(normed(hidden_in, gain_attn))
    queries = low_back(product(normed_in, w_query) + b_query)
    keys = low_back(product(normed_in, w_key) + b_key)
    values = low(low_back(product(normed_in, w_value) + b_value))
    queries = low(rotate(queries.reshape(length, HEADS, HEAD_DIM), cosine, sine))
    keys = low(rotate(keys.reshape(length, KV_HEADS, HEAD_DIM), cosine, sine))
    per_head = (queries.reshape(length, KV_HEADS, groups, HEAD_DIM).transpose(1, 0, 2, 3), keys.transpose(1, 0, 2), values.reshape(length, KV_HEADS, HEAD_DIM).transpose(1, 0, 2))

    def one_head(inputs_head):
        return attend(inputs_head[0], inputs_head[1], inputs_head[2], segs)
    mixed_heads = lax.map(jax.checkpoint(one_head), per_head)
    attended = low(low_back(mixed_heads.transpose(1, 0, 2, 3).reshape(length, HEADS * HEAD_DIM)))
    middle = hidden_in + live * low_back(product(attended, w_output))
    normed_mid = low(normed(middle, gain_mlp))
    gate = low_back(product(normed_mid, w_gate))
    upward = low_back(product(normed_mid, w_up))
    activ = low(jax.nn.silu(gate) * upward)
    return middle + live * low_back(product(activ, w_down))

def reference(tokens, segments, cotangent, w_query, w_key, w_value, w_output, w_gate, w_up, w_down, b_query, b_key, b_value, gain_attn, gain_mlp):
    devices_all = TOKENS // TOK_DEV
    hidden_all = tokens.astype(jnp.float32).reshape(devices_all, TOK_DEV, D)
    cotan_all = cotangent.astype(jnp.float32).reshape(devices_all, TOK_DEV, D)
    seg_all = segments.astype(jnp.int32).reshape(devices_all, TOK_DEV)
    params = (w_query.astype(jnp.float32), w_key.astype(jnp.float32), w_value.astype(jnp.float32), w_output.astype(jnp.float32), w_gate.astype(jnp.float32), w_up.astype(jnp.float32), w_down.astype(jnp.float32), b_query.astype(jnp.float32), b_key.astype(jnp.float32), b_value.astype(jnp.float32), gain_attn.astype(jnp.float32), gain_mlp.astype(jnp.float32))

    def device_step(summed, inputs_dev):
        hidden_dev, segs_dev, cotan_dev = inputs_dev

        def forward(hidden_val, *weights):
            return block_layer(hidden_val, segs_dev, *weights)
        result, pullback = jax.vjp(forward, hidden_dev, *params)
        gradients = pullback(cotan_dev)
        summed = tuple((before + gradient for before, gradient in zip(summed, gradients[1:])))
        return (summed, (result.astype(jnp.bfloat16), gradients[0]))
    zeros_all = tuple((jnp.zeros_like(param) for param in params))
    totals, (outputs, input_grads) = lax.scan(device_step, zeros_all, (hidden_all, seg_all, cotan_all))
    return (outputs.reshape(TOKENS, D), input_grads.reshape(TOKENS, D), totals[0], totals[1], totals[2], totals[3], totals[4], totals[5], totals[6], totals[7], totals[8], totals[9], totals[10], totals[11])
```

```python
import functools

import jax
import jax.numpy as jnp
from jax import lax
from jax.sharding import PartitionSpec as P

HEAD_DIM = 64


EPSILON = 1e-06
THETA = 1000000.0
NEGATIVE = -1e30


def positions(segs):
    length = segs.shape[0]
    index = jnp.arange(length, dtype=jnp.int32)
    before = jnp.concatenate([jnp.full((1,), -2, dtype=jnp.int32), segs[:-1]])
    starts = lax.cummax(jnp.where(segs != before, index, jnp.zeros_like(index)), axis=0)
    return (index - starts).astype(jnp.float32)


def rope_tables(segs, head_dim):
    halfway = head_dim // 2
    inverse = THETA ** (-(jnp.arange(halfway, dtype=jnp.float32) * 2.0 / head_dim))
    angles = positions(segs)[:, None] * inverse[None, :]
    return (jnp.cos(angles), jnp.sin(angles))


def rotate(values, cosine, sine):
    halfway = values.shape[-1] // 2
    first = values[..., :halfway]
    second = values[..., halfway:]
    cosine = cosine[:, None, :]
    sine = sine[:, None, :]
    return jnp.concatenate(
        [first * cosine - second * sine, second * cosine + first * sine], axis=-1
    )


def normed(values, gain):
    scale = lax.rsqrt(jnp.mean(values * values, axis=-1, keepdims=True) + EPSILON)
    return values * scale * gain


def forward_product(left, right):
    return jnp.dot(left, right, preferred_element_type=jnp.float32)


def contract_rows(left, right):
    return lax.dot_general(
        left, right, (((0,), (0,)), ((), ())), preferred_element_type=jnp.float32
    )


def contract_cols(left, right):
    return lax.dot_general(
        left, right, (((1,), (1,)), ((), ())), preferred_element_type=jnp.float32
    )


def block_mask(segs, row_start, block_rows):
    length = segs.shape[0]
    row_index = row_start + jnp.arange(block_rows, dtype=jnp.int32)
    col_index = jnp.arange(length, dtype=jnp.int32)
    return (segs[:, None] == segs[None, :]) & (row_index[:, None] >= col_index[None, :])


def head_forward(queries, keys, values, segs, block_rows):
    length, groups, head_dim = queries.shape
    scale = head_dim ** (-0.5)
    block_count = length // block_rows
    starts = jnp.arange(block_count, dtype=jnp.int32) * block_rows
    blocks = queries.reshape(block_count, block_rows, groups, head_dim)

    def one_block(inputs_blk):
        query_blk, row_start = inputs_blk
        raw = jnp.einsum("tgd,sd->gts", query_blk, keys, preferred_element_type=jnp.float32) * scale
        allowed = block_mask(segs, row_start, block_rows)
        scores = jnp.where(allowed[None], raw, NEGATIVE)
        row_max = jnp.max(scores, axis=-1, keepdims=True)
        exponent = jnp.exp(scores - row_max)
        row_total = jnp.sum(exponent, axis=-1, keepdims=True)
        probs = (exponent / row_total).astype(jnp.bfloat16)
        attended = jnp.einsum("gts,sd->tgd", probs, values, preferred_element_type=jnp.float32)
        return (attended, (row_max + jnp.log(row_total))[..., 0])

    attended_all, log_totals = lax.map(one_block, (blocks, starts))
    return (attended_all.reshape(length, groups, head_dim), log_totals)


def head_backward(queries, keys, values, grad_heads, log_totals, segs, block_rows):
    length, groups, head_dim = queries.shape
    scale = head_dim ** (-0.5)
    block_count = length // block_rows
    starts = jnp.arange(block_count, dtype=jnp.int32) * block_rows
    query_blocks = queries.reshape(block_count, block_rows, groups, head_dim)
    grad_blocks = grad_heads.reshape(block_count, block_rows, groups, head_dim)

    def one_block(carry, inputs_blk):
        key_grad, value_grad = carry
        query_blk, grad_blk, log_blk, row_start = inputs_blk
        raw = jnp.einsum("tgd,sd->gts", query_blk, keys, preferred_element_type=jnp.float32) * scale
        allowed = block_mask(segs, row_start, block_rows)
        scores = jnp.where(allowed[None], raw, NEGATIVE)
        probs = jnp.exp(scores - log_blk[..., None])
        value_grad = value_grad + jnp.einsum(
            "gts,tgd->sd", probs.astype(jnp.bfloat16), grad_blk, preferred_element_type=jnp.float32
        )
        prob_grad = jnp.einsum("tgd,sd->gts", grad_blk, values, preferred_element_type=jnp.float32)
        score_grad = (
            probs * (prob_grad - jnp.sum(prob_grad * probs, axis=-1, keepdims=True))
        ).astype(jnp.bfloat16)
        query_grad = (
            jnp.einsum("gts,sd->tgd", score_grad, keys, preferred_element_type=jnp.float32) * scale
        )
        key_grad = (
            key_grad
            + jnp.einsum("gts,tgd->sd", score_grad, query_blk, preferred_element_type=jnp.float32)
            * scale
        )
        return ((key_grad, value_grad), query_grad)

    zeros_head = jnp.zeros((length, head_dim), jnp.float32)
    (key_grad, value_grad), query_grads = lax.scan(
        one_block, (zeros_head, zeros_head), (query_blocks, grad_blocks, log_totals, starts)
    )
    return (query_grads.reshape(length, groups, head_dim), key_grad, value_grad)


def swapped(value, axis, bit, size):
    step = 1 << bit
    return lax.ppermute(value, axis, [(at, at ^ step) for at in range(size)])


def chosen(parts, at):
    return lax.dynamic_index_in_dim(parts, at, 0, keepdims=False)


def added(left, right):
    return (left.astype(jnp.float32) + right.astype(jnp.float32)).astype(jnp.bfloat16)


def ordered(own, other, bit):
    return jnp.where(bit == 0, jnp.stack([own, other]), jnp.stack([other, own]))


class Group:
    def __init__(self, size, replicas):
        self.size = size
        self.replicas = replicas
        self.at = lax.axis_index("fsdp")
        self.core = lax.axis_index("rep") & 1
        self.pair = size == 2 and replicas % 2 == 0

    def swap(self, value):
        return swapped(value, "fsdp", 0, 2)

    def rows_of_other(self, rows):
        half = rows.shape[0] // 2
        mine = lax.dynamic_slice_in_dim(rows, self.core * half, half, 0)
        got = self.swap(mine)
        both = ordered(got, swapped(got, "rep", 0, self.replicas), self.core)
        return both.reshape(rows.shape)

    def whole_rows(self, rows):
        if not self.pair:
            return lax.all_gather(rows, "fsdp", axis=0, tiled=True)
        both = ordered(rows, self.rows_of_other(rows), self.at)
        return both.reshape((2 * rows.shape[0],) + rows.shape[1:])

    def whole_vector(self, vector):
        if not self.pair:
            return lax.all_gather(vector, "fsdp", axis=0, tiled=False)
        return ordered(vector, self.swap(vector), self.at)

    def my_columns(self, rows):
        if not self.pair:
            return lax.all_to_all(rows, "fsdp", 1, 0, tiled=True)
        width = rows.shape[1] // 2
        mine = lax.dynamic_slice_in_dim(rows, self.at * width, width, 1)
        theirs = lax.dynamic_slice_in_dim(rows, (1 - self.at) * width, width, 1)
        both = ordered(mine, self.rows_of_other(theirs), self.at)
        return both.reshape(2 * rows.shape[0], width)

    def all_tokens(self, value):
        if not self.pair:
            return lax.all_gather(value, "fsdp", axis=0, tiled=True)
        return jnp.concatenate([value, self.swap(value)])

    def own_tokens(self, partial):
        if not self.pair:
            return lax.psum_scatter(partial, "fsdp", scatter_dimension=0, tiled=True)
        length = partial.shape[0] // 2
        got = self.swap(partial[length:].astype(jnp.bfloat16))
        return partial[:length] + got.astype(jnp.float32)

    def sum_parts(self, parts):
        if not self.pair:
            return lax.psum_scatter(parts, "fsdp", scatter_dimension=0, tiled=False)
        got = self.swap(chosen(parts, 1 - self.at))
        return added(chosen(parts, self.at), got)

    def exchange_parts(self, parts):
        if not self.pair:
            return lax.all_to_all(parts, "fsdp", 0, 0, tiled=True)
        got = self.swap(chosen(parts, 1 - self.at))
        return ordered(chosen(parts, self.at), got, self.at)


class Replicas:
    def __init__(self, size):
        self.size = size
        self.at = lax.axis_index("rep")
        self.bits = size.bit_length() - 1
        self.far = list(range(1, self.bits))

    def bit(self, bit):
        return (self.at >> bit) & 1

    def scatter(self, parts, bit):
        mine = self.bit(bit)
        got = swapped(chosen(parts, 1 - mine), "rep", bit, self.size)
        return added(chosen(parts, mine), got)

    def gather(self, value, bit):
        return ordered(value, swapped(value, "rep", bit, self.size), self.bit(bit))

    def scatter_all(self, parts, order):
        for bit in order:
            parts = self.scatter(parts.reshape((2, parts.shape[0] // 2) + parts.shape[1:]), bit)
        return parts.reshape(parts.shape[1:])

    def gather_all(self, value, order):
        value = value[None]
        for bit in reversed(order):
            value = self.gather(value, bit)
            value = value.reshape((value.shape[0] * value.shape[1],) + value.shape[2:])
        return value

    def both_cores(self, value):
        return self.gather(value, 0)


def shards(
    tokens,
    segments,
    cotangent,
    w_query,
    w_key,
    w_value,
    w_output,
    w_gate,
    w_up,
    w_down,
    b_query,
    b_key,
    b_value,
    gain_attn,
    gain_mlp,
    group_size,
    replica_count,
):
    group = Group(group_size, replica_count)
    replicas = Replicas(replica_count)
    far = replicas.far
    near_first = [far[1], far[0]] + far[2:]
    eighth = 1 << len(far)
    width = tokens.shape[1]
    rows_own = w_query.shape[0]
    qw, kw = w_query.shape[1], w_key.shape[1]
    vectors = group.whole_vector(
        jnp.concatenate([b_query, b_key, b_value, gain_attn, gain_mlp])
    ).astype(jnp.float32)
    cuts = [0]
    for part in (b_query, b_key, b_value, gain_attn, gain_mlp):
        cuts.append(cuts[-1] + part.shape[0])
    bias_query, bias_key, bias_value, full_gain_attn, full_gain_mlp = (
        vectors[:, low:high].reshape(-1) for low, high in zip(cuts[:-1], cuts[1:])
    )
    full_qkv = group.whole_rows(jnp.concatenate([w_query, w_key, w_value], axis=1))
    full_output = group.whole_rows(w_output)
    part_gate = group.my_columns(w_gate)
    part_up = group.my_columns(w_up)
    length = tokens.shape[0]
    heads = qw // HEAD_DIM
    kv_heads = kw // HEAD_DIM
    groups = heads // kv_heads
    block_rows = min(512, length)
    hidden_in = tokens.astype(jnp.float32)
    grad_in = cotangent.astype(jnp.float32)
    live = (segments >= 0).astype(jnp.float32)[:, None]
    mlp_grad = (live * grad_in).astype(jnp.bfloat16)
    mlp_grad_all = group.all_tokens(mlp_grad)
    cosine, sine = rope_tables(segments, HEAD_DIM)
    normed_low = normed(hidden_in, full_gain_attn).astype(jnp.bfloat16)
    pre = forward_product(normed_low, full_qkv)
    query_pre = pre[:, :qw] + bias_query
    key_pre = pre[:, qw : qw + kw] + bias_key
    value_low = (pre[:, qw + kw :] + bias_value).astype(jnp.bfloat16)
    query_rot = (
        rotate(query_pre.reshape(length, heads, HEAD_DIM), cosine, sine)
        .astype(jnp.bfloat16)
        .reshape(length, kv_heads, groups, HEAD_DIM)
    )
    key_rot = rotate(key_pre.reshape(length, kv_heads, HEAD_DIM), cosine, sine).astype(jnp.bfloat16)
    value_heads = value_low.reshape(length, kv_heads, HEAD_DIM)
    head_outputs = []
    head_logs = []
    for kv_head in range(kv_heads):
        attended, log_totals = head_forward(
            query_rot[:, kv_head],
            key_rot[:, kv_head],
            value_heads[:, kv_head],
            segments,
            block_rows,
        )
        head_outputs.append(attended)
        head_logs.append(log_totals)
    attended_low = (
        jnp.stack(head_outputs, axis=1).reshape(length, heads * HEAD_DIM).astype(jnp.bfloat16)
    )
    middle = hidden_in + live * forward_product(attended_low, full_output)
    mid_low = normed(middle, full_gain_mlp).astype(jnp.bfloat16)

    mid_all = group.all_tokens(mid_low)
    gate = forward_product(mid_all, part_gate)
    upward = forward_product(mid_all, part_up)
    activ_grad = contract_cols(mlp_grad_all, w_down)
    sigmoid_gate = jax.nn.sigmoid(gate)
    activ_low = (gate * sigmoid_gate * upward).astype(jnp.bfloat16)
    gate_grad = (activ_grad * upward * sigmoid_gate * (1.0 + gate * (1.0 - sigmoid_gate))).astype(
        jnp.bfloat16
    )
    up_grad = (activ_grad * gate * sigmoid_gate).astype(jnp.bfloat16)

    grad_down = contract_rows(activ_low, mlp_grad_all).astype(jnp.bfloat16)
    down_half = replicas.scatter(grad_down.reshape(2, -1, width), 0)
    down_piece = replicas.scatter_all(down_half.reshape(eighth, -1, width), far)
    grad_pair = jnp.stack(
        [
            contract_rows(mid_all, gate_grad).astype(jnp.bfloat16),
            contract_rows(mid_all, up_grad).astype(jnp.bfloat16),
        ]
    )
    hidden = grad_pair.shape[2]
    cut = -(-hidden // 256) * 128
    pair_pieces = []
    for low, high, order in ((0, cut, near_first), (cut, hidden, far)):
        summed = replicas.scatter(grad_pair[:, :, low:high], 0)
        summed = summed.reshape(group_size, eighth, rows_own // eighth, high - low)
        piece = replicas.scatter_all(summed.transpose(1, 0, 2, 3), order)
        piece = group.exchange_parts(piece)
        pair_pieces.append((piece, order))
    mid_norm_grad = group.own_tokens(
        contract_cols(gate_grad, part_gate) + contract_cols(up_grad, part_up)
    )
    output = (middle + live * group.own_tokens(forward_product(activ_low, w_down))).astype(
        jnp.bfloat16
    )
    mid_pull = jax.vjp(normed, middle, full_gain_mlp)[1]
    middle_grad, gain_mlp_grad = mid_pull(mid_norm_grad)
    middle_grad = middle_grad + grad_in
    attn_grad = (live * middle_grad).astype(jnp.bfloat16)
    grad_output = contract_rows(attended_low, attn_grad)
    attended_grad = (
        contract_cols(attn_grad, full_output)
        .astype(jnp.bfloat16)
        .reshape(length, kv_heads, groups, HEAD_DIM)
    )
    query_parts = []
    key_parts = []
    value_parts = []
    for kv_head in range(kv_heads):
        query_part, key_part, value_part = head_backward(
            query_rot[:, kv_head],
            key_rot[:, kv_head],
            value_heads[:, kv_head],
            attended_grad[:, kv_head],
            head_logs[kv_head],
            segments,
            block_rows,
        )
        query_parts.append(query_part)
        key_parts.append(key_part)
        value_parts.append(value_part)
    query_grad_rot = jnp.stack(query_parts, axis=1).reshape(length, heads, HEAD_DIM)
    key_grad_rot = jnp.stack(key_parts, axis=1)
    qkv_grad = jnp.concatenate(
        [
            rotate(query_grad_rot, cosine, -sine).reshape(length, qw),
            rotate(key_grad_rot, cosine, -sine).reshape(length, kw),
            jnp.stack(value_parts, axis=1).reshape(length, kw),
        ],
        axis=1,
    ).astype(jnp.bfloat16)
    grad_qkv = contract_rows(normed_low, qkv_grad)
    bias_grad = jnp.sum(qkv_grad.astype(jnp.float32), axis=0)
    in_norm_grad = contract_cols(qkv_grad, full_qkv)
    in_pull = jax.vjp(normed, hidden_in, full_gain_attn)[1]
    input_grad, gain_attn_grad = in_pull(in_norm_grad)
    input_grad = input_grad + middle_grad

    small = jnp.concatenate(
        [
            part.reshape(group_size, -1)
            for part in (
                bias_grad[:qw],
                bias_grad[qw : qw + kw],
                bias_grad[qw + kw :],
                gain_attn_grad,
                gain_mlp_grad,
            )
        ],
        axis=1,
    ).astype(jnp.bfloat16)
    columns = grad_qkv.shape[1] + qw
    extra = 16
    small = jnp.pad(small, ((0, 0), (0, extra * columns - small.shape[1])))
    attn_all = jnp.concatenate(
        [
            jnp.concatenate([grad_qkv, grad_output], axis=1)
            .astype(jnp.bfloat16)
            .reshape(group_size, rows_own, columns),
            small.reshape(group_size, extra, columns),
        ],
        axis=1,
    )
    attn_half = replicas.scatter(
        attn_all.reshape(group_size, 2, (rows_own + extra) // 2, columns).transpose(1, 0, 2, 3), 0
    )
    attn_own = group.sum_parts(attn_half)
    attn_cols = attn_own.reshape(-1, eighth, columns // eighth).transpose(1, 0, 2)
    attn_piece = replicas.scatter_all(attn_cols, far)

    down_sum = replicas.both_cores(replicas.gather_all(down_piece, far))
    shard_down = down_sum.reshape(-1, width).astype(jnp.float32)
    halves = []
    for piece, order in pair_pieces:
        full = replicas.both_cores(replicas.gather_all(piece, order))
        halves.append(full.transpose(0, 1, 3, 2, 4).reshape(2, rows_own, group_size, -1))
    shard_pair = jnp.concatenate(halves, axis=3).reshape(2, rows_own, -1)
    shard_gate = shard_pair[0].astype(jnp.float32)
    shard_up = shard_pair[1].astype(jnp.float32)
    attn_sum = replicas.both_cores(replicas.gather_all(attn_piece, far))
    attn_sum = attn_sum.transpose(0, 2, 1, 3).reshape(rows_own + extra, columns).astype(jnp.float32)
    shard_query = attn_sum[:rows_own, :qw]
    shard_key = attn_sum[:rows_own, qw : qw + kw]
    shard_value = attn_sum[:rows_own, qw + kw : qw + 2 * kw]
    shard_output = attn_sum[:rows_own, qw + 2 * kw :]
    vector_sum = attn_sum[rows_own:].reshape(-1)
    shard_vectors = tuple(vector_sum[low:high] for low, high in zip(cuts[:-1], cuts[1:]))
    return (
        output,
        input_grad,
        shard_query,
        shard_key,
        shard_value,
        shard_output,
        shard_gate,
        shard_up,
        shard_down,
    ) + shard_vectors


def solution(mesh):
    placed = (
        P(("rep", "fsdp"), None),
        P(("rep", "fsdp")),
        P(("rep", "fsdp"), None),
        P("fsdp", None),
        P("fsdp", None),
        P("fsdp", None),
        P("fsdp", None),
        P("fsdp", None),
        P("fsdp", None),
        P("fsdp", None),
        P("fsdp"),
        P("fsdp"),
        P("fsdp"),
        P("fsdp"),
        P("fsdp"),
    )
    return jax.shard_map(
        functools.partial(
            shards, group_size=mesh.shape["fsdp"], replica_count=mesh.shape["rep"]
        ),
        mesh=mesh,
        in_specs=placed,
        out_specs=(
            P(("rep", "fsdp"), None),
            P(("rep", "fsdp"), None),
            P("fsdp", None),
            P("fsdp", None),
            P("fsdp", None),
            P("fsdp", None),
            P("fsdp", None),
            P("fsdp", None),
            P("fsdp", None),
            P("fsdp"),
            P("fsdp"),
            P("fsdp"),
            P("fsdp"),
            P("fsdp"),
        ),
        check_vma=False,
    )
```

```python
import functools

import jax
import jax.numpy as jnp
from jax import lax
from jax.experimental import pallas as pl
from jax.experimental.pallas import tpu as pltpu
from jax.sharding import PartitionSpec as P

HEAD_DIM = 64


EPSILON = 1e-06
THETA = 1000000.0
NEGATIVE = -1e30


def positions(segs):
    length = segs.shape[0]
    index = jnp.arange(length, dtype=jnp.int32)
    before = jnp.concatenate([jnp.full((1,), -2, dtype=jnp.int32), segs[:-1]])
    starts = lax.cummax(jnp.where(segs != before, index, jnp.zeros_like(index)), axis=0)
    return (index - starts).astype(jnp.float32)


def rope_tables(segs, head_dim):
    halfway = head_dim // 2
    inverse = THETA ** (-(jnp.arange(halfway, dtype=jnp.float32) * 2.0 / head_dim))
    angles = positions(segs)[:, None] * inverse[None, :]
    return (jnp.cos(angles), jnp.sin(angles))


def normed(values, gain):
    scale = lax.rsqrt(jnp.mean(values * values, axis=-1, keepdims=True) + EPSILON)
    return values * scale * gain


def forward_product(left, right):
    return jnp.dot(left, right, preferred_element_type=jnp.float32)


def contract_rows(left, right):
    return lax.dot_general(
        left, right, (((0,), (0,)), ((), ())), preferred_element_type=jnp.float32
    )


def contract_cols(left, right):
    return lax.dot_general(
        left, right, (((1,), (1,)), ((), ())), preferred_element_type=jnp.float32
    )


LANES = 128


def lane_index(shape):
    return lax.broadcasted_iota(jnp.int32, shape, len(shape) - 1)


def swapped_halves(values):
    half = HEAD_DIM // 2
    lanes = lane_index(values.shape)
    return jnp.where(
        lanes % HEAD_DIM < half,
        pltpu.roll(values, LANES - half, 1),
        pltpu.roll(values, half, 1),
    )


def doubled(pair, head):
    lanes = lane_index(pair.shape)
    wide = pair.astype(jnp.float32)
    other = pltpu.roll(wide, HEAD_DIM, 1)
    return jnp.where((lanes < HEAD_DIM) == (head == 0), wide, other).astype(jnp.bfloat16)


def one_head(pair, parity):
    lanes = lane_index(pair.shape)
    return jnp.where((lanes < HEAD_DIM) == (parity == 0), pair, jnp.zeros_like(pair))


def mask_bias(segs_col, segs_row, row_start):
    rows, keys = segs_col.shape[0], segs_row.shape[1]
    row_index = row_start + lax.broadcasted_iota(jnp.int32, (rows, keys), 0)
    col_index = lax.broadcasted_iota(jnp.int32, (rows, keys), 1)
    allowed = (segs_col == segs_row) & (row_index >= col_index)
    return jnp.where(allowed, 0.0, NEGATIVE).astype(jnp.float32)


def is_live(segs):
    return jnp.where(segs >= 0, 1.0, 0.0)


def double_keys(key_rot, value_low, keys_two, values_two):
    for kv_head in range(2):
        keys_two[kv_head] = doubled(key_rot[...], kv_head)
        values_two[kv_head] = doubled(value_low[...], kv_head)


def attend_rows(
    row_start, key_count, groups, pairs, segs_col, segs_row, query_rot, keys_two, values_two,
    bias, attended, logs, tokens, w_output, gain, middle, mid_low,
):
    rows = attended.shape[0]
    bias[...] = mask_bias(
        segs_col[row_start : row_start + rows], segs_row[:, :key_count], row_start
    )
    logs[...] = jnp.zeros_like(logs)

    def one_pair(pair, carry):
        cols = pl.ds(pl.multiple_of(pair * LANES, LANES), LANES)
        queries = query_rot[row_start : row_start + rows, cols]
        results = []
        log_all = logs[...]
        lanes = lane_index(log_all.shape)
        for parity in range(2):
            head = 2 * pair + parity
            kv_head = head // groups
            query = one_head(queries, parity) * jnp.asarray(HEAD_DIM**-0.5, jnp.bfloat16)
            scores = contract_cols(query, keys_two[kv_head, :key_count]) + bias[...]
            row_max = jnp.max(scores, axis=-1, keepdims=True)
            exponent = jnp.exp(scores - row_max)
            row_total = jnp.sum(exponent, axis=-1, keepdims=True)
            probs = (exponent * (1.0 / row_total)).astype(jnp.bfloat16)
            results.append(forward_product(probs, values_two[kv_head, :key_count]))
            log_all = jnp.where(lanes == head, row_max + jnp.log(row_total), log_all)
        logs[...] = log_all
        attended[:, cols] = jnp.where(
            lane_index(results[0].shape) < HEAD_DIM, results[0], results[1]
        ).astype(jnp.bfloat16)
        return carry

    lax.fori_loop(0, pairs, one_pair, 0)
    mixed = forward_product(attended[...], w_output[...])
    here = slice(row_start, row_start + rows)
    total = tokens[here, :].astype(jnp.float32) + is_live(segs_col[here, :]) * mixed
    middle[...] = total
    mid_low[...] = normed(total, gain[...]).astype(jnp.bfloat16)


def early_kernel(
    groups, pairs, normed_low, w_qkv, bias_qkv, cosine, sine, segs_col, segs_row, tokens,
    w_output, gain, query_rot, key_rot, value_low, attended, logs, middle, mid_low,
    bias, keys_two, values_two,
):
    def project(pair):
        cols = pl.ds(pl.multiple_of(pair * LANES, LANES), LANES)
        return forward_product(normed_low[...], w_qkv[:, cols]) + bias_qkv[:, cols]

    def turned(values):
        return (values * cosine[...] + swapped_halves(values) * sine[...]).astype(jnp.bfloat16)

    def query_pair(pair, carry):
        cols = pl.ds(pl.multiple_of(pair * LANES, LANES), LANES)
        query_rot[:, cols] = turned(project(pair))
        return carry

    lax.fori_loop(0, pairs, query_pair, 0)
    key_rot[...] = turned(project(pairs))
    value_low[...] = project(pairs + 1).astype(jnp.bfloat16)
    double_keys(key_rot, value_low, keys_two, values_two)
    attend_rows(
        0, attended.shape[0], groups, pairs, segs_col, segs_row, query_rot, keys_two, values_two,
        bias, attended, logs, tokens, w_output, gain, middle, mid_low,
    )


def late_kernel(
    groups, pairs, query_rot, key_rot, value_low, segs_col, segs_row, tokens,
    w_output, gain, attended, logs, middle, mid_low, bias, keys_two, values_two,
):
    double_keys(key_rot, value_low, keys_two, values_two)
    rows = attended.shape[0]
    attend_rows(
        rows, 2 * rows, groups, pairs, segs_col, segs_row, query_rot, keys_two, values_two,
        bias, attended, logs, tokens, w_output, gain, middle, mid_low,
    )


def call(kernel, out_shape, scratch, cost, operands):
    return pl.pallas_call(
        kernel,
        out_shape=[jax.ShapeDtypeStruct(shape, kind) for shape, kind in out_shape],
        in_specs=[pl.BlockSpec(memory_space=pltpu.VMEM)] * len(operands),
        out_specs=[pl.BlockSpec(memory_space=pltpu.VMEM)] * len(out_shape),
        scratch_shapes=[pltpu.VMEM(shape, kind) for shape, kind in scratch],
        compiler_params=pltpu.CompilerParams(vmem_limit_bytes=56 * 2**20),
        cost_estimate=pl.CostEstimate(flops=cost, bytes_accessed=cost // 300, transcendentals=0),
    )(*operands)


def attention_shapes(length, w_output, kw):
    queries, width = w_output.shape
    rows = length // 2
    low, wide = jnp.bfloat16, jnp.float32
    half_out = [
        ((rows, queries), low), ((rows, LANES), wide), ((rows, width), wide), ((rows, width), low)
    ]
    return rows, queries, queries // kw, queries // LANES, half_out, [((2, length, LANES), low)] * 2


def attention_early(
    normed_low, w_qkv, bias_qkv, cosine, sine, segs_col, segs_row, tokens, w_output, gain
):
    length = tokens.shape[0]
    kw = (w_qkv.shape[1] - w_output.shape[0]) // 2
    rows, queries, groups, pairs, half_out, scratch = attention_shapes(length, w_output, kw)
    whole = [((length, columns), jnp.bfloat16) for columns in (queries, kw, kw)]
    query_rot, key_rot, value_low, *early = call(
        functools.partial(early_kernel, groups, pairs),
        whole + half_out,
        [((rows, rows), jnp.float32)] + scratch,
        2 * 10**9,
        (normed_low, w_qkv, bias_qkv, cosine, sine, segs_col, segs_row, tokens, w_output, gain),
    )
    return query_rot, key_rot, value_low, early


def attention_late(query_rot, key_rot, value_low, segs_col, segs_row, tokens, w_output, gain):
    length = tokens.shape[0]
    rows, _, groups, pairs, half_out, scratch = attention_shapes(
        length, w_output, key_rot.shape[1]
    )
    return call(
        functools.partial(late_kernel, groups, pairs),
        half_out,
        [((rows, length), jnp.float32)] + scratch,
        2 * 10**9,
        (query_rot, key_rot, value_low, segs_col, segs_row, tokens, w_output, gain),
    )


def norm_pull(values, gain, grad):
    scale = lax.rsqrt(jnp.mean(values * values, axis=-1, keepdims=True) + EPSILON)
    unit = values * scale
    inner = grad * gain
    pull = scale * (inner - unit * jnp.mean(inner * unit, axis=-1, keepdims=True))
    return pull, jnp.sum(grad * unit, axis=0, keepdims=True)


def backward_kernel(
    groups, pairs, mid_early, mid_late, norm_grad, cotangent, gain_mlp, w_output,
    att_early, att_late, log_early, log_late, query_rot, key_rot, value_low, segs_col, segs_row,
    cosine, sine, normed_low, w_qkv, tokens, gain_attn,
    grad_qkv, grad_output, bias_grad, attn_gain_grad, mlp_gain_grad, input_grad,
    attn_grad, attended_grad, low_grads, bias, keys_two, values_two, key_grad, value_grad,
):
    rows = mid_early.shape[0]
    length = 2 * rows
    parts = ((0, mid_early, att_early, log_early), (rows, mid_late, att_late, log_late))
    gain_sum = jnp.zeros(mlp_gain_grad.shape, jnp.float32)
    for start, middle, _, _ in parts:
        here = slice(start, start + rows)
        pull, gain_part = norm_pull(middle[...], gain_mlp[...], norm_grad[here, :])
        gain_sum = gain_sum + gain_part
        total = cotangent[here, :].astype(jnp.float32) + pull
        input_grad[here, :] = total
        attn_grad[here, :] = (is_live(segs_col[here, :]) * total).astype(jnp.bfloat16)
        bias[here, :] = mask_bias(segs_col[here], segs_row[...], start)
    mlp_gain_grad[...] = gain_sum
    double_keys(key_rot, value_low, keys_two, values_two)
    key_grad[...] = jnp.zeros_like(key_grad)
    value_grad[...] = jnp.zeros_like(value_grad)
    bias_grad[...] = jnp.zeros_like(bias_grad)
    for start in range(0, length, rows):
        here = slice(start, start + rows)
        attended_grad[here, :] = contract_cols(attn_grad[here, :], w_output[...]).astype(
            jnp.bfloat16
        )

    def turned_back(values, here):
        return values * cosine[here, :] - swapped_halves(values) * sine[here, :]

    def one_pair(pair, carry):
        cols = pl.ds(pl.multiple_of(pair * LANES, LANES), LANES)
        column_sum = jnp.zeros((1, LANES), jnp.float32)
        out_grad = jnp.zeros((LANES, attn_grad.shape[1]), jnp.float32)
        for start, _, attended, logs in parts:
            here = slice(start, start + rows)
            keys = start + rows
            out_grad = out_grad + contract_rows(attended[:, cols], attn_grad[here, :])
            queries = query_rot[here, cols]
            grads = attended_grad[here, cols]
            log_all = logs[...]
            lanes = lane_index(log_all.shape)
            results = []
            for parity in range(2):
                head = 2 * pair + parity
                kv_head = head // groups
                query = one_head(queries, parity) * jnp.asarray(HEAD_DIM**-0.5, jnp.bfloat16)
                grad = one_head(grads, parity)
                log_total = jnp.sum(
                    jnp.where(lanes == head, log_all, 0.0), axis=-1, keepdims=True
                )
                scores = contract_cols(query, keys_two[kv_head, :keys]) + bias[here, :keys]
                probs = jnp.exp(scores - log_total)
                prob_grad = contract_cols(grad, values_two[kv_head, :keys])
                inner = jnp.sum(prob_grad * probs, axis=-1, keepdims=True)
                score_grad = (probs * (prob_grad - inner)).astype(jnp.bfloat16)
                value_grad[kv_head, :keys] += contract_rows(probs.astype(jnp.bfloat16), grad)
                key_grad[kv_head, :keys] += contract_rows(score_grad, query)
                results.append(
                    forward_product(score_grad, keys_two[kv_head, :keys]) * HEAD_DIM**-0.5
                )
            query_grad = jnp.where(
                lane_index(results[0].shape) < HEAD_DIM, results[0], results[1]
            )
            low = turned_back(query_grad, here).astype(jnp.bfloat16)
            low_grads[here, cols] = low
            column_sum = column_sum + jnp.sum(low.astype(jnp.float32), axis=0, keepdims=True)
        bias_grad[:, cols] = column_sum
        grad_output[cols, :] = out_grad.astype(jnp.bfloat16)
        return carry

    lax.fori_loop(0, pairs, one_pair, 0)

    def folded(pair_sums):
        both = [pair_sums[at] + pltpu.roll(pair_sums[at], HEAD_DIM, 1) for at in range(2)]
        return jnp.where(lane_index(both[0].shape) < HEAD_DIM, both[0], both[1])

    everywhere = slice(0, length)
    key_low = turned_back(folded(key_grad), everywhere).astype(jnp.bfloat16)
    value_grad_low = folded(value_grad).astype(jnp.bfloat16)
    for at, low in ((pairs, key_low), (pairs + 1, value_grad_low)):
        cols = slice(at * LANES, (at + 1) * LANES)
        low_grads[:, cols] = low
        bias_grad[:, cols] = jnp.sum(low.astype(jnp.float32), axis=0, keepdims=True)

    def weight_rows(block, carry):
        cols = pl.ds(pl.multiple_of(block * LANES, LANES), LANES)
        grad_qkv[cols, :] = contract_rows(normed_low[:, cols], low_grads[...]).astype(jnp.bfloat16)
        return carry

    lax.fori_loop(0, normed_low.shape[1] // LANES, weight_rows, 0)
    gain_sum = jnp.zeros(attn_gain_grad.shape, jnp.float32)
    for start in range(0, length, rows):
        here = slice(start, start + rows)
        norm_in = contract_cols(low_grads[here, :], w_qkv[...])
        pull, gain_part = norm_pull(tokens[here, :].astype(jnp.float32), gain_attn[...], norm_in)
        gain_sum = gain_sum + gain_part
        input_grad[here, :] += pull
    attn_gain_grad[...] = gain_sum


def attention_backward(
    early, late, norm_grad, cotangent, gain_mlp, w_output, query_rot, key_rot, value_low,
    segs_col, segs_row, cosine, sine, normed_low, w_qkv, tokens, gain_attn,
):
    length, width = tokens.shape
    queries = w_output.shape[0]
    columns = w_qkv.shape[1]
    kw = (columns - queries) // 2
    low, wide = jnp.bfloat16, jnp.float32
    return call(
        functools.partial(backward_kernel, queries // kw, queries // LANES),
        [
            ((width, columns), low),
            ((queries, width), low),
            ((1, columns), wide),
            ((1, width), wide),
            ((1, width), wide),
            ((length, width), wide),
        ],
        [
            ((length, width), low),
            ((length, queries), low),
            ((length, columns), low),
            ((length, length), wide),
            ((2, length, LANES), low),
            ((2, length, LANES), low),
            ((2, length, LANES), wide),
            ((2, length, LANES), wide),
        ],
        10**9,
        (early[2], late[2], norm_grad, cotangent, gain_mlp, w_output, early[0], late[0],
         early[1], late[1], query_rot, key_rot, value_low, segs_col, segs_row, cosine, sine,
         normed_low, w_qkv, tokens, gain_attn),
    )


def swapped(value, axis, bit, size):
    step = 1 << bit
    return lax.ppermute(value, axis, [(at, at ^ step) for at in range(size)])


def chosen(parts, at):
    return lax.dynamic_index_in_dim(parts, at, 0, keepdims=False)


def added(left, right):
    return (left.astype(jnp.float32) + right.astype(jnp.float32)).astype(jnp.bfloat16)


def ordered(own, other, bit):
    return jnp.where(bit == 0, jnp.stack([own, other]), jnp.stack([other, own]))


def column_cuts(columns):
    step = 4 * LANES
    return [(low, min(low + step, columns)) for low in range(0, columns, step)]


def hidden_kernel(carries, mid_low, mlp_grad, w_gate, w_up, w_down, *refs):
    activ, gate_grad, up_grad = refs[carries:]
    for low, high in column_cuts(w_gate.shape[1]):
        gate = forward_product(mid_low[...], w_gate[:, low:high])
        upward = forward_product(mid_low[...], w_up[:, low:high])
        grad = contract_cols(mlp_grad[...], w_down[low:high, :])
        sigmoid = jax.nn.sigmoid(gate)
        silu = gate * sigmoid
        activ[:, low:high] = (silu * upward).astype(jnp.bfloat16)
        gate_grad[:, low:high] = (grad * upward * (sigmoid + silu * (1.0 - sigmoid))).astype(
            jnp.bfloat16
        )
        up_grad[:, low:high] = (grad * silu).astype(jnp.bfloat16)


def whole_block(array):
    return pl.BlockSpec(array.shape, lambda at: (0,) * array.ndim)


def row_block(array, rows, start=0):
    return pl.BlockSpec((rows, array.shape[1]), lambda at: (at + start, 0))


def grid_call(kernel, grid, operands, in_specs, out_shape, out_specs, flops, aliases=None):
    return pl.pallas_call(
        kernel,
        grid=(grid,),
        out_shape=out_shape,
        in_specs=in_specs,
        out_specs=out_specs,
        input_output_aliases=aliases or {},
        compiler_params=pltpu.CompilerParams(vmem_limit_bytes=56 * 2**20),
        cost_estimate=pl.CostEstimate(flops=flops, bytes_accessed=10**6, transcendentals=0),
    )(*operands)


def hidden_part(mid_low, mlp_grad, w_gate, w_up, w_down, total, start, carried):
    rows = 256
    count = mid_low.shape[0] // rows
    first = start // rows
    shapes = [jax.ShapeDtypeStruct((total, w_gate.shape[1]), jnp.bfloat16)] * 3
    return grid_call(
        functools.partial(hidden_kernel, len(carried)),
        count,
        [mid_low, mlp_grad, w_gate, w_up, w_down] + list(carried),
        [row_block(mid_low, rows), row_block(mlp_grad, rows)]
        + [whole_block(weight) for weight in (w_gate, w_up, w_down)]
        + [pl.BlockSpec(memory_space=pl.ANY)] * len(carried),
        shapes,
        [row_block(shape, rows, first) for shape in shapes],
        10**9,
        {5 + at: at for at in range(len(carried))},
    )


def norm_part_kernel(gate_grad, up_grad, w_gate, w_up, out):
    out[...] = (
        contract_cols(gate_grad[...], w_gate[...]) + contract_cols(up_grad[...], w_up[...])
    ).astype(out.dtype)


def out_part_kernel(activ, w_down, out):
    out[...] = forward_product(activ[...], w_down[...]).astype(out.dtype)


def token_product(kernel, activs, weights, width, start, count, kind):
    rows = 256
    out = jax.ShapeDtypeStruct((count, width), kind)
    return grid_call(
        kernel,
        count // rows,
        list(activs) + list(weights),
        [row_block(activ, rows, start // rows) for activ in activs]
        + [whole_block(weight) for weight in weights],
        out,
        row_block(out, rows),
        10**9,
    )


def together(*values):
    return lax.optimization_barrier(values)


class Group:
    def __init__(self, size, replicas):
        self.size = size
        self.replicas = replicas
        self.at = lax.axis_index("fsdp")
        self.replica = lax.axis_index("rep")
        self.pair = size == 2 and replicas % 2 == 0

    def swap(self, value):
        return swapped(value, "fsdp", 0, 2)

    def fetched(self, rows, bits):
        start, count = 0, rows.shape[0]
        for bit in bits:
            count //= 2
            start = start + ((self.replica >> bit) & 1) * count
        return self.swap(lax.dynamic_slice_in_dim(rows, start, count, 0))

    def shared(self, part, bits):
        for bit in reversed(bits):
            other = swapped(part, "rep", bit, self.replicas)
            part = ordered(part, other, (self.replica >> bit) & 1)
            part = part.reshape((-1,) + part.shape[2:])
        return part

    def joined(self, own, other):
        return ordered(own, other, self.at).reshape((-1,) + own.shape[1:])

    def whole_vector(self, vector):
        if not self.pair:
            return lax.all_gather(vector, "fsdp", axis=0, tiled=False)
        return ordered(vector, self.swap(vector), self.at)

    def columns(self, rows, owner):
        width = rows.shape[1] // 2
        return lax.dynamic_slice_in_dim(rows, owner * width, width, 1)

    def plain_weights(self, qkv, w_output, w_gate, w_up):
        return (
            lax.all_gather(qkv, "fsdp", axis=0, tiled=True),
            lax.all_gather(w_output, "fsdp", axis=0, tiled=True),
            lax.all_to_all(w_gate, "fsdp", 1, 0, tiled=True),
            lax.all_to_all(w_up, "fsdp", 1, 0, tiled=True),
        )

    def all_tokens(self, value):
        return lax.all_gather(value, "fsdp", axis=0, tiled=True)

    def own_tokens(self, partial):
        return lax.psum_scatter(partial, "fsdp", scatter_dimension=0, tiled=True)

    def sum_parts(self, parts):
        if not self.pair:
            return lax.psum_scatter(parts, "fsdp", scatter_dimension=0, tiled=False)
        got = self.swap(chosen(parts, 1 - self.at))
        return added(chosen(parts, self.at), got)

    def exchange_parts(self, parts):
        if not self.pair:
            return lax.all_to_all(parts, "fsdp", 0, 0, tiled=True)
        got = self.swap(chosen(parts, 1 - self.at))
        return ordered(chosen(parts, self.at), got, self.at)


class Replicas:
    def __init__(self, size):
        self.size = size
        self.at = lax.axis_index("rep")
        self.bits = size.bit_length() - 1
        self.far = list(range(1, self.bits))

    def bit(self, bit):
        return (self.at >> bit) & 1

    def swap_core(self, value):
        return swapped(value, "rep", 0, self.size)

    def scatter(self, parts, bit):
        mine = self.bit(bit)
        got = swapped(chosen(parts, 1 - mine), "rep", bit, self.size)
        return added(chosen(parts, mine), got)

    def gather(self, value, bit):
        return ordered(value, swapped(value, "rep", bit, self.size), self.bit(bit))

    def first(self, parts, order):
        if not order:
            return parts
        return self.scatter(parts.reshape((2, -1) + parts.shape[1:]), order[0])

    def scatter_all(self, parts, order):
        for at in range(len(order)):
            parts = self.first(parts, order[at:])
        return parts.reshape(parts.shape[1:])

    def gather_all(self, value, order):
        value = value[None]
        for bit in reversed(order):
            value = self.gather(value, bit)
            value = value.reshape((value.shape[0] * value.shape[1],) + value.shape[2:])
        return value


def shards(
    tokens,
    segments,
    cotangent,
    w_query,
    w_key,
    w_value,
    w_output,
    w_gate,
    w_up,
    w_down,
    b_query,
    b_key,
    b_value,
    gain_attn,
    gain_mlp,
    group_size,
    replica_count,
):
    group = Group(group_size, replica_count)
    replicas = Replicas(replica_count)
    far = replicas.far
    near_first = [far[1], far[0]] + far[2:]
    eighth = 1 << len(far)
    width = tokens.shape[1]
    rows_own = w_query.shape[0]
    qw, kw = w_query.shape[1], w_key.shape[1]
    vectors = group.whole_vector(
        jnp.concatenate([b_query, b_key, b_value, gain_attn, gain_mlp])
    ).astype(jnp.float32)
    cuts = [0]
    for part in (b_query, b_key, b_value, gain_attn, gain_mlp):
        cuts.append(cuts[-1] + part.shape[0])
    bias_query, bias_key, bias_value, full_gain_attn, full_gain_mlp = (
        vectors[:, low:high].reshape(-1) for low, high in zip(cuts[:-1], cuts[1:])
    )
    qkv = jnp.concatenate([w_query, w_key, w_value], axis=1)
    live = (segments >= 0).astype(jnp.float32)[:, None]
    mlp_grad = (live * cotangent.astype(jnp.float32)).astype(jnp.bfloat16)
    cosine, sine = rope_tables(segments, HEAD_DIM)
    copies = LANES // HEAD_DIM
    cosine = jnp.concatenate([cosine, cosine] * copies, axis=1)
    sine = jnp.concatenate([-sine, sine] * copies, axis=1)
    segs_col, segs_row = segments[:, None], segments[None, :]
    normed_low = normed(tokens.astype(jnp.float32), full_gain_attn).astype(jnp.bfloat16)
    gain_attn_row, gain_mlp_row = full_gain_attn[None, :], full_gain_mlp[None, :]
    bias_row = jnp.concatenate([bias_query, bias_key, bias_value])[None, :]
    if group.pair:
        cores = [0]
        chips = [0, 1] if replica_count % 4 == 0 else [0]
        got_qkv, got_output = group.fetched(qkv, cores), group.fetched(w_output, cores)
        got_qkv, got_output, w_gate, w_up = together(got_qkv, got_output, w_gate, w_up)
        full_qkv = group.joined(qkv, group.shared(got_qkv, cores))
        full_output = group.joined(w_output, group.shared(got_output, cores))
        got_gate = group.fetched(group.columns(w_gate, 1 - group.at), chips)
        got_up = group.fetched(group.columns(w_up, 1 - group.at), chips)
    else:
        full_qkv, full_output, part_gate, part_up = group.plain_weights(
            qkv, w_output, w_gate, w_up
        )
    query_rot, key_rot, value_low, early = attention_early(
        normed_low, full_qkv, bias_row, cosine, sine, segs_col, segs_row, tokens, full_output,
        gain_mlp_row,
    )
    if group.pair:
        query_rot, early, got_gate, got_up, mlp_grad = together(
            query_rot, early, got_gate, got_up, mlp_grad
        )
        got_gate, got_up = group.shared(got_gate, chips[1:]), group.shared(got_up, chips[1:])
        others = [group.swap(early[3])]
        mlp_other = group.swap(mlp_grad)
    late = attention_late(
        query_rot, key_rot, value_low, segs_col, segs_row, tokens, full_output, gain_mlp_row
    )
    mid_own = jnp.concatenate([early[3], late[3]])
    length = tokens.shape[0]
    if group.pair:
        late, got_gate, got_up, others = together(late, got_gate, got_up, others)
        others.append(group.swap(late[3]))
        got_gate, got_up = group.shared(got_gate, cores), group.shared(got_up, cores)
        part_gate = group.joined(group.columns(w_gate, group.at), got_gate)
        part_up = group.joined(group.columns(w_up, group.at), got_up)
        hidden = hidden_part(
            mid_own, mlp_grad, part_gate, part_up, w_down, group_size * length, 0, ()
        )
        hidden, others, mlp_other = together(hidden, others, mlp_other)
        mid_other = jnp.concatenate(others)
        activ_low, gate_grad, up_grad = hidden_part(
            mid_other, mlp_other, part_gate, part_up, w_down, group_size * length, length, hidden
        )
        mid_all = jnp.concatenate([mid_own, mid_other])
        mlp_grad_all = jnp.concatenate([mlp_grad, mlp_other])
    else:
        mid_all = group.all_tokens(mid_own)
        mlp_grad_all = group.all_tokens(mlp_grad)
        activ_low, gate_grad, up_grad = hidden_part(
            mid_all, mlp_grad_all, part_gate, part_up, w_down, group_size * length, 0, ()
        )
    middle = jnp.concatenate([early[2], late[2]])

    back_weights, out_weights = (part_gate, part_up), (w_down,)
    back = (gate_grad, up_grad)
    everyone = group_size * length
    if group.pair:
        norm_other = token_product(
            norm_part_kernel, back, back_weights, width, length, length, jnp.bfloat16
        )
        norm_other, activ_low, back = together(norm_other, activ_low, back)
    grad_down = contract_rows(activ_low, mlp_grad_all).astype(jnp.bfloat16)
    grad_down, back = together(grad_down, back)
    gate_grad, up_grad = back
    grad_gate = contract_rows(mid_all, gate_grad).astype(jnp.bfloat16)
    grad_up = contract_rows(mid_all, up_grad).astype(jnp.bfloat16)
    down = replicas.scatter(grad_down.reshape(2, -1, width), 0).reshape(eighth, -1, width)
    grad_gate, grad_up, down, back, activ_low = together(
        grad_gate, grad_up, down, back, activ_low
    )
    hidden_units = grad_gate.shape[1]
    cut = -(-hidden_units // 256) * 128
    core = replicas.bit(0)
    pair_parts = []
    for low, high in ((0, cut), (cut, hidden_units)):
        gate_range, up_range = grad_gate[:, low:high], grad_up[:, low:high]
        got = replicas.swap_core(jnp.where(core == 0, up_range, gate_range))
        summed = added(jnp.where(core == 0, gate_range, up_range), got)
        summed = summed.reshape(group_size, eighth, rows_own // eighth, high - low)
        pair_parts.append(summed.transpose(1, 0, 2, 3))
    first, second = pair_parts
    down = replicas.first(down, far)
    if group.pair:
        norm_grad = token_product(
            norm_part_kernel, back, back_weights, width, 0, length, jnp.float32
        )
        norm_grad = norm_grad + group.swap(norm_other).astype(jnp.float32)
        out_other = token_product(
            out_part_kernel, (activ_low,), out_weights, width, length, length, jnp.bfloat16
        )
    else:
        norm_grad = group.own_tokens(
            token_product(norm_part_kernel, back, back_weights, width, 0, everyone, jnp.float32)
        )
        out_other = token_product(
            out_part_kernel, (activ_low,), out_weights, width, 0, everyone, jnp.float32
        )
    norm_grad, down, first, second, out_other, activ_low = together(
        norm_grad, down, first, second, out_other, activ_low
    )
    grad_qkv, grad_output, bias_grad, gain_attn_grad, gain_mlp_grad, input_grad = (
        attention_backward(
            early, late, norm_grad, cotangent, gain_mlp_row, full_output, query_rot, key_rot,
            value_low, segs_col, segs_row, cosine, sine, normed_low, full_qkv, tokens,
            gain_attn_row,
        )
    )
    down = replicas.first(down, far[1:])
    first = replicas.first(first, near_first)
    second = replicas.first(second, far)
    if group.pair:
        out_sum = token_product(
            out_part_kernel, (activ_low,), out_weights, width, 0, length, jnp.float32
        )
        out_sum = out_sum + group.swap(out_other).astype(jnp.float32)
    else:
        out_sum = group.own_tokens(out_other)
    grad_qkv, grad_output, bias_grad, gain_attn_grad, gain_mlp_grad, down, first, second = together(
        grad_qkv, grad_output, bias_grad, gain_attn_grad, gain_mlp_grad, down, first, second
    )
    output = (middle + live * out_sum).astype(jnp.bfloat16)

    small = jnp.concatenate(
        [
            part.reshape(group_size, -1)
            for part in (
                bias_grad[0, :qw],
                bias_grad[0, qw : qw + kw],
                bias_grad[0, qw + kw :],
                gain_attn_grad,
                gain_mlp_grad,
            )
        ],
        axis=1,
    ).astype(jnp.bfloat16)
    columns = grad_qkv.shape[1] + qw
    unit = 16 * eighth
    extra = -(-(rows_own + 16) // unit) * unit - rows_own
    small = jnp.pad(small, ((0, 0), (0, extra * columns - small.shape[1])))
    attn_all = jnp.concatenate(
        [
            jnp.concatenate([grad_qkv, grad_output], axis=1)
            .astype(jnp.bfloat16)
            .reshape(group_size, rows_own, columns),
            small.reshape(group_size, extra, columns),
        ],
        axis=1,
    )
    attn = replicas.scatter(
        attn_all.reshape(group_size, 2, (rows_own + extra) // 2, columns).transpose(1, 0, 2, 3), 0
    )
    down = replicas.scatter_all(down, far[2:])
    first = group.exchange_parts(replicas.scatter_all(first, near_first[1:]))
    second = group.exchange_parts(replicas.scatter_all(second, far[1:]))
    attn = group.sum_parts(attn).reshape(eighth, -1, columns)
    attn = replicas.scatter_all(attn, far)
    down = replicas.gather(replicas.gather_all(down, far), 0)
    first = replicas.gather_all(first, near_first)
    second = replicas.gather_all(second, far)
    attn = replicas.gather_all(attn, far)
    shard_down = down.reshape(-1, width).astype(jnp.float32)
    gate_parts = [[] for _ in range(group_size)]
    up_parts = [[] for _ in range(group_size)]
    for mine in (first, second):
        got = replicas.swap_core(mine)
        for matrix, parts in (
            (jnp.where(core == 0, mine, got), gate_parts),
            (jnp.where(core == 0, got, mine), up_parts),
        ):
            for sender in range(group_size):
                parts[sender].append(matrix[:, sender].reshape(rows_own, -1))
    shard_gate, shard_up = (
        jnp.concatenate(sum(parts, []), axis=1).astype(jnp.float32)
        for parts in (gate_parts, up_parts)
    )
    attn_sum = replicas.gather(attn, 0).reshape(rows_own + extra, columns).astype(jnp.float32)
    shard_query = attn_sum[:rows_own, :qw]
    shard_key = attn_sum[:rows_own, qw : qw + kw]
    shard_value = attn_sum[:rows_own, qw + kw : qw + 2 * kw]
    shard_output = attn_sum[:rows_own, qw + 2 * kw :]
    vector_sum = attn_sum[rows_own:].reshape(-1)
    shard_vectors = tuple(vector_sum[low:high] for low, high in zip(cuts[:-1], cuts[1:]))
    return (
        output,
        input_grad,
        shard_query,
        shard_key,
        shard_value,
        shard_output,
        shard_gate,
        shard_up,
        shard_down,
    ) + shard_vectors


def solution(mesh):
    placed = (
        P(("rep", "fsdp"), None),
        P(("rep", "fsdp")),
        P(("rep", "fsdp"), None),
        P("fsdp", None),
        P("fsdp", None),
        P("fsdp", None),
        P("fsdp", None),
        P("fsdp", None),
        P("fsdp", None),
        P("fsdp", None),
        P("fsdp"),
        P("fsdp"),
        P("fsdp"),
        P("fsdp"),
        P("fsdp"),
    )
    return jax.shard_map(
        functools.partial(
            shards, group_size=mesh.shape["fsdp"], replica_count=mesh.shape["rep"]
        ),
        mesh=mesh,
        in_specs=placed,
        out_specs=(
            P(("rep", "fsdp"), None),
            P(("rep", "fsdp"), None),
            P("fsdp", None),
            P("fsdp", None),
            P("fsdp", None),
            P("fsdp", None),
            P("fsdp", None),
            P("fsdp", None),
            P("fsdp", None),
            P("fsdp"),
            P("fsdp"),
            P("fsdp"),
            P("fsdp"),
            P("fsdp"),
        ),
        check_vma=False,
    )
```

```python
import functools

import jax
import jax.numpy as jnp
from jax import lax
from jax.experimental import pallas as pl
from jax.experimental.pallas import tpu as pltpu
from jax.sharding import PartitionSpec as P

HEAD_DIM = 64


EPSILON = 1e-06
THETA = 1000000.0
NEGATIVE = -1e30


def positions(segs):
    length = segs.shape[0]
    index = jnp.arange(length, dtype=jnp.int32)
    before = jnp.concatenate([jnp.full((1,), -2, dtype=jnp.int32), segs[:-1]])
    starts = lax.cummax(jnp.where(segs != before, index, jnp.zeros_like(index)), axis=0)
    return (index - starts).astype(jnp.float32)


def rope_tables(segs, head_dim):
    halfway = head_dim // 2
    inverse = THETA ** (-(jnp.arange(halfway, dtype=jnp.float32) * 2.0 / head_dim))
    angles = positions(segs)[:, None] * inverse[None, :]
    return (jnp.cos(angles), jnp.sin(angles))


def normed(values, gain):
    scale = lax.rsqrt(jnp.mean(values * values, axis=-1, keepdims=True) + EPSILON)
    return values * scale * gain


def forward_product(left, right):
    return jnp.dot(left, right, preferred_element_type=jnp.float32)


def contract_rows(left, right):
    return lax.dot_general(
        left, right, (((0,), (0,)), ((), ())), preferred_element_type=jnp.float32
    )


def contract_cols(left, right):
    return lax.dot_general(
        left, right, (((1,), (1,)), ((), ())), preferred_element_type=jnp.float32
    )


LANES = 128


def lane_index(shape):
    return lax.broadcasted_iota(jnp.int32, shape, len(shape) - 1)


def swapped_halves(values):
    half = HEAD_DIM // 2
    lanes = lane_index(values.shape)
    return jnp.where(
        lanes % HEAD_DIM < half,
        pltpu.roll(values, LANES - half, 1),
        pltpu.roll(values, half, 1),
    )


def doubled(pair, head):
    lanes = lane_index(pair.shape)
    wide = pair.astype(jnp.float32)
    other = pltpu.roll(wide, HEAD_DIM, 1)
    return jnp.where((lanes < HEAD_DIM) == (head == 0), wide, other).astype(jnp.bfloat16)


def one_head(pair, parity):
    lanes = lane_index(pair.shape)
    return jnp.where((lanes < HEAD_DIM) == (parity == 0), pair, jnp.zeros_like(pair))


def mask_bias(key_segs, row_segs, row_start):
    keys, rows = key_segs.shape[0], row_segs.shape[1]
    key_index = lax.broadcasted_iota(jnp.int32, (keys, rows), 0)
    row_index = row_start + lax.broadcasted_iota(jnp.int32, (keys, rows), 1)
    allowed = (key_segs == row_segs) & (row_index >= key_index)
    return jnp.where(allowed, 0.0, NEGATIVE).astype(jnp.float32)


def is_live(segs):
    return jnp.where(segs >= 0, 1.0, 0.0)


def turned_over(values):
    return jnp.transpose(values.astype(jnp.float32)).astype(jnp.bfloat16)


def one_of_pair(first, second):
    rows = lax.broadcasted_iota(jnp.int32, first.shape, 0)
    return jnp.where(rows < HEAD_DIM, first, second)


def attend_rows(
    row_start, key_count, groups, pairs, segs_col, segs_row, query_rot, key_rot, value_low,
    bias, keys_two, values_over, attended, logs, tokens, w_output, gain, middle, mid_low,
):
    rows = attended.shape[0]
    for kv_head in range(2):
        keys_two[kv_head] = doubled(key_rot[:key_count, :], kv_head)
        values_over[kv_head] = turned_over(doubled(value_low[:key_count, :], kv_head))
    bias[...] = mask_bias(
        segs_col[:key_count], segs_row[:, row_start : row_start + rows], row_start
    )

    def one_pair(pair, carry):
        cols = pl.ds(pl.multiple_of(pair * LANES, LANES), LANES)
        queries = query_rot[row_start : row_start + rows, cols]
        results = []
        for parity in range(2):
            head = 2 * pair + parity
            kv_head = head // groups
            query = one_head(queries, parity) * jnp.asarray(HEAD_DIM**-0.5, jnp.bfloat16)
            scores = contract_cols(keys_two[kv_head], query) + bias[...]
            row_max = jnp.max(scores, axis=0, keepdims=True)
            exponent = jnp.exp(scores - row_max)
            row_total = jnp.sum(exponent, axis=0, keepdims=True)
            probs = (exponent * (1.0 / row_total)).astype(jnp.bfloat16)
            results.append(forward_product(values_over[kv_head], probs))
            logs[pl.ds(head, 1), :] = row_max + jnp.log(row_total)
        attended[:, cols] = jnp.transpose(one_of_pair(*results)).astype(jnp.bfloat16)
        return carry

    lax.fori_loop(0, pairs, one_pair, 0)
    mixed = forward_product(attended[...], w_output[...])
    here = slice(row_start, row_start + rows)
    total = tokens[here, :].astype(jnp.float32) + is_live(segs_col[here, :]) * mixed
    middle[...] = total
    mid_low[...] = normed(total, gain[...]).astype(jnp.bfloat16)


def early_kernel(
    groups, pairs, normed_low, w_qkv, bias_qkv, cosine, sine, segs_col, segs_row, tokens,
    w_output, gain, query_rot, key_rot, value_low, attended, logs, middle, mid_low,
    bias, keys_two, values_over,
):
    def project(pair):
        cols = pl.ds(pl.multiple_of(pair * LANES, LANES), LANES)
        return forward_product(normed_low[...], w_qkv[:, cols]) + bias_qkv[:, cols]

    def turned(values):
        return (values * cosine[...] + swapped_halves(values) * sine[...]).astype(jnp.bfloat16)

    def query_pair(pair, carry):
        cols = pl.ds(pl.multiple_of(pair * LANES, LANES), LANES)
        query_rot[:, cols] = turned(project(pair))
        return carry

    lax.fori_loop(0, pairs, query_pair, 0)
    key_rot[...] = turned(project(pairs))
    value_low[...] = project(pairs + 1).astype(jnp.bfloat16)
    attend_rows(
        0, attended.shape[0], groups, pairs, segs_col, segs_row, query_rot, key_rot, value_low,
        bias, keys_two, values_over, attended, logs, tokens, w_output, gain, middle, mid_low,
    )


def late_kernel(
    groups, pairs, query_rot, key_rot, value_low, segs_col, segs_row, tokens,
    w_output, gain, attended, logs, middle, mid_low, bias, keys_two, values_over,
):
    rows = attended.shape[0]
    attend_rows(
        rows, 2 * rows, groups, pairs, segs_col, segs_row, query_rot, key_rot, value_low,
        bias, keys_two, values_over, attended, logs, tokens, w_output, gain, middle, mid_low,
    )


def call(kernel, out_shape, scratch, cost, operands):
    return pl.pallas_call(
        kernel,
        out_shape=[jax.ShapeDtypeStruct(shape, kind) for shape, kind in out_shape],
        in_specs=[pl.BlockSpec(memory_space=pltpu.VMEM)] * len(operands),
        out_specs=[pl.BlockSpec(memory_space=pltpu.VMEM)] * len(out_shape),
        scratch_shapes=[pltpu.VMEM(shape, kind) for shape, kind in scratch],
        compiler_params=pltpu.CompilerParams(vmem_limit_bytes=56 * 2**20),
        cost_estimate=pl.CostEstimate(flops=cost, bytes_accessed=cost // 300, transcendentals=0),
    )(*operands)


def attention_shapes(length, key_count, w_output, kw):
    queries, width = w_output.shape
    rows = length // 2
    heads = -(-queries // HEAD_DIM // 8) * 8
    low, wide = jnp.bfloat16, jnp.float32
    half_out = [
        ((rows, queries), low), ((heads, rows), wide), ((rows, width), wide), ((rows, width), low)
    ]
    scratch = [
        ((key_count, rows), wide), ((2, key_count, LANES), low), ((2, LANES, key_count), low)
    ]
    return queries, queries // kw, queries // LANES, half_out, scratch


def attention_early(
    normed_low, w_qkv, bias_qkv, cosine, sine, segs_col, segs_row, tokens, w_output, gain
):
    length = tokens.shape[0]
    kw = (w_qkv.shape[1] - w_output.shape[0]) // 2
    queries, groups, pairs, half_out, scratch = attention_shapes(
        length, length // 2, w_output, kw
    )
    whole = [((length, columns), jnp.bfloat16) for columns in (queries, kw, kw)]
    query_rot, key_rot, value_low, *early = call(
        functools.partial(early_kernel, groups, pairs),
        whole + half_out,
        scratch,
        2 * 10**9,
        (normed_low, w_qkv, bias_qkv, cosine, sine, segs_col, segs_row, tokens, w_output, gain),
    )
    return query_rot, key_rot, value_low, early


def attention_late(query_rot, key_rot, value_low, segs_col, segs_row, tokens, w_output, gain):
    length = tokens.shape[0]
    _, groups, pairs, half_out, scratch = attention_shapes(
        length, length, w_output, key_rot.shape[1]
    )
    return call(
        functools.partial(late_kernel, groups, pairs),
        half_out,
        scratch,
        2 * 10**9,
        (query_rot, key_rot, value_low, segs_col, segs_row, tokens, w_output, gain),
    )


def norm_pull(values, gain, grad):
    scale = lax.rsqrt(jnp.mean(values * values, axis=-1, keepdims=True) + EPSILON)
    unit = values * scale
    inner = grad * gain
    pull = scale * (inner - unit * jnp.mean(inner * unit, axis=-1, keepdims=True))
    return pull, jnp.sum(grad * unit, axis=0, keepdims=True)


def backward_kernel(
    groups, pairs, devices, mid_early, mid_late, norm_own, norm_got, cotangent, gain_mlp, w_output,
    att_early, att_late, log_early, log_late, query_rot, key_rot, value_low, segs_col, segs_row,
    cosine, sine, normed_low, w_qkv, tokens, gain_attn,
    sums, input_grad, attn_grad, attended_grad, low_grads, bias, keys_two, keys_over, values_two, key_grad, value_grad,
    qkv_sums, out_sums,
):
    rows = mid_early.shape[0]
    length = 2 * rows
    parts = ((0, mid_early, att_early, log_early), (rows, mid_late, att_late, log_late))
    width, columns = w_qkv.shape
    own = width // devices
    padded = sums.shape[0] // devices

    def sum_row(row, first, value):
        low = value.astype(jnp.bfloat16)
        for device in range(devices):
            at = device * padded + own + row
            sums[at : at + 1, first : first + low.shape[1]] = low

    for device in range(devices):
        at = device * padded + own
        sums[at : at + padded - own, :] = jnp.zeros((padded - own, sums.shape[1]), jnp.bfloat16)
    gain_sum = jnp.zeros(gain_mlp.shape, jnp.float32)
    for start, middle, _, _ in parts:
        here = slice(start, start + rows)
        pull, gain_part = norm_pull(
            middle[...],
            gain_mlp[...],
            norm_own[here, :] + norm_got[here, :].astype(jnp.float32),
        )
        gain_sum = gain_sum + gain_part
        total = cotangent[here, :].astype(jnp.float32) + pull
        input_grad[here, :] = total
        attn_grad[here, :] = (is_live(segs_col[here, :]) * total).astype(jnp.bfloat16)
        bias[: start + rows, here] = mask_bias(segs_col[: start + rows], segs_row[:, here], start)
    sum_row(1, 0, gain_sum)
    for kv_head in range(2):
        keys_two[kv_head] = doubled(key_rot[...], kv_head)
        keys_over[kv_head] = turned_over(keys_two[kv_head])
        values_two[kv_head] = doubled(value_low[...], kv_head)
    key_grad[...] = jnp.zeros_like(key_grad)
    value_grad[...] = jnp.zeros_like(value_grad)
    for start in range(0, length, rows):
        here = slice(start, start + rows)
        attended_grad[here, :] = contract_cols(attn_grad[here, :], w_output[...]).astype(
            jnp.bfloat16
        )

    def turned_back(values, here):
        return values * cosine[here, :] - swapped_halves(values) * sine[here, :]

    def one_pair(pair, carry):
        cols = pl.ds(pl.multiple_of(pair * LANES, LANES), LANES)
        out_grad = jnp.zeros((LANES, attn_grad.shape[1]), jnp.float32)
        for start, _, attended, logs in parts:
            here = slice(start, start + rows)
            keys = start + rows
            out_grad = out_grad + contract_rows(attended[:, cols], attn_grad[here, :])
            queries = query_rot[here, cols]
            grads = attended_grad[here, cols]
            results = []
            for parity in range(2):
                head = 2 * pair + parity
                kv_head = head // groups
                query = one_head(queries, parity) * jnp.asarray(HEAD_DIM**-0.5, jnp.bfloat16)
                grad = one_head(grads, parity)
                scores = contract_cols(keys_two[kv_head, :keys], query) + bias[:keys, here]
                probs = jnp.exp(scores - logs[pl.ds(head, 1), :])
                prob_grad = contract_cols(values_two[kv_head, :keys], grad)
                inner = jnp.sum(prob_grad * probs, axis=0, keepdims=True)
                score_grad = (probs * (prob_grad - inner)).astype(jnp.bfloat16)
                value_grad[kv_head, :keys] += forward_product(probs.astype(jnp.bfloat16), grad)
                key_grad[kv_head, :keys] += forward_product(score_grad, query)
                results.append(forward_product(keys_over[kv_head, :, :keys], score_grad))
            query_grad = jnp.transpose(one_of_pair(*results)) * HEAD_DIM**-0.5
            low = turned_back(query_grad, here).astype(jnp.bfloat16)
            low_grads[here, cols] = low
        out_sums[cols, :] = out_grad.astype(jnp.bfloat16)
        return carry

    lax.fori_loop(0, pairs, one_pair, 0)

    def folded(pair_sums):
        both = [pair_sums[at] + pltpu.roll(pair_sums[at], HEAD_DIM, 1) for at in range(2)]
        return jnp.where(lane_index(both[0].shape) < HEAD_DIM, both[0], both[1])

    everywhere = slice(0, length)
    key_low = turned_back(folded(key_grad), everywhere).astype(jnp.bfloat16)
    value_grad_low = folded(value_grad).astype(jnp.bfloat16)
    for at, low in ((pairs, key_low), (pairs + 1, value_grad_low)):
        cols = slice(at * LANES, (at + 1) * LANES)
        low_grads[:, cols] = low
    sum_row(0, 0, jnp.sum(low_grads[...].astype(jnp.float32), axis=0, keepdims=True))

    def weight_rows(block, carry):
        cols = pl.ds(pl.multiple_of(block * LANES, LANES), LANES)
        qkv_sums[cols, :] = contract_rows(normed_low[:, cols], low_grads[...]).astype(jnp.bfloat16)
        return carry

    lax.fori_loop(0, width // LANES, weight_rows, 0)
    for device in range(devices):
        here = slice(device * padded, device * padded + own)
        there = slice(device * own, (device + 1) * own)
        sums[here, :columns] = qkv_sums[there, :]
        sums[here, columns:] = out_sums[there, :]
    gain_sum = jnp.zeros(gain_attn.shape, jnp.float32)
    for start in range(0, length, rows):
        here = slice(start, start + rows)
        norm_in = contract_cols(low_grads[here, :], w_qkv[...])
        pull, gain_part = norm_pull(tokens[here, :].astype(jnp.float32), gain_attn[...], norm_in)
        gain_sum = gain_sum + gain_part
        input_grad[here, :] += pull
    sum_row(0, columns, gain_sum)


def attention_backward(
    devices, padded, early, late, norm_own, norm_got, cotangent, gain_mlp, w_output, query_rot, key_rot, value_low,
    segs_col, segs_row, cosine, sine, normed_low, w_qkv, tokens, gain_attn,
):
    length, width = tokens.shape
    queries = w_output.shape[0]
    columns = w_qkv.shape[1]
    kw = (columns - queries) // 2
    low, wide = jnp.bfloat16, jnp.float32
    return call(
        functools.partial(backward_kernel, queries // kw, queries // LANES, devices),
        [((devices * padded, columns + width), low), ((length, width), wide)],
        [
            ((length, width), low),
            ((length, queries), low),
            ((length, columns), low),
            ((length, length), wide),
            ((2, length, LANES), low),
            ((2, LANES, length), low),
            ((2, length, LANES), low),
            ((2, length, LANES), wide),
            ((2, length, LANES), wide),
            ((width, columns), low),
            ((queries, width), low),
        ],
        10**9,
        (early[2], late[2], norm_own, norm_got, cotangent, gain_mlp, w_output, early[0], late[0],
         early[1], late[1], query_rot, key_rot, value_low, segs_col, segs_row, cosine, sine,
         normed_low, w_qkv, tokens, gain_attn),
    )


def swapped(value, axis, bit, size):
    step = 1 << bit
    return lax.ppermute(value, axis, [(at, at ^ step) for at in range(size)])


def chosen(parts, at):
    return lax.dynamic_index_in_dim(parts, at, 0, keepdims=False)


def added(left, right):
    return (left.astype(jnp.float32) + right.astype(jnp.float32)).astype(jnp.bfloat16)


def ordered(own, other, bit):
    return jnp.where(bit == 0, jnp.stack([own, other]), jnp.stack([other, own]))


def column_cuts(columns):
    step = 4 * LANES
    return [(low, min(low + step, columns)) for low in range(0, columns, step)]


def hidden_kernel(carries, mid_low, mlp_grad, w_gate, w_up, w_down, *refs):
    activ, gate_grad, up_grad = refs[carries:]
    for low, high in column_cuts(w_gate.shape[1]):
        gate = forward_product(mid_low[...], w_gate[:, low:high])
        upward = forward_product(mid_low[...], w_up[:, low:high])
        grad = contract_cols(mlp_grad[...], w_down[low:high, :])
        sigmoid = jax.nn.sigmoid(gate)
        silu = gate * sigmoid
        activ[:, low:high] = (silu * upward).astype(jnp.bfloat16)
        gate_grad[:, low:high] = (grad * upward * (sigmoid + silu * (1.0 - sigmoid))).astype(
            jnp.bfloat16
        )
        up_grad[:, low:high] = (grad * silu).astype(jnp.bfloat16)


def whole_block(array):
    return pl.BlockSpec(array.shape, lambda at: (0,) * array.ndim)


def row_block(array, rows, start=0):
    return pl.BlockSpec((rows, array.shape[1]), lambda at: (at + start, 0))


def grid_call(kernel, grid, operands, in_specs, out_shape, out_specs, flops, aliases=None):
    return pl.pallas_call(
        kernel,
        grid=(grid,),
        out_shape=out_shape,
        in_specs=in_specs,
        out_specs=out_specs,
        input_output_aliases=aliases or {},
        compiler_params=pltpu.CompilerParams(vmem_limit_bytes=56 * 2**20),
        cost_estimate=pl.CostEstimate(flops=flops, bytes_accessed=10**6, transcendentals=0),
    )(*operands)


def hidden_part(mid_low, mlp_grad, w_gate, w_up, w_down, total, start, carried):
    rows = 256
    count = mid_low.shape[0] // rows
    first = start // rows
    shapes = [jax.ShapeDtypeStruct((total, w_gate.shape[1]), jnp.bfloat16)] * 3
    return grid_call(
        functools.partial(hidden_kernel, len(carried)),
        count,
        [mid_low, mlp_grad, w_gate, w_up, w_down] + list(carried),
        [row_block(mid_low, rows), row_block(mlp_grad, rows)]
        + [whole_block(weight) for weight in (w_gate, w_up, w_down)]
        + [pl.BlockSpec(memory_space=pl.ANY)] * len(carried),
        shapes,
        [row_block(shape, rows, first) for shape in shapes],
        10**9,
        {5 + at: at for at in range(len(carried))},
    )


def norm_part_kernel(gate_grad, up_grad, w_gate, w_up, first, second):
    value = contract_cols(gate_grad[...], w_gate[...]) + contract_cols(up_grad[...], w_up[...])
    two_parts(value, first, second)


def out_part_kernel(activ, w_down, first, second):
    two_parts(forward_product(activ[...], w_down[...]), first, second)


def two_parts(value, first, second):
    at, half = pl.program_id(0), pl.num_programs(0) // 2

    @pl.when(at < half)
    def _():
        first[...] = value.astype(first.dtype)

    @pl.when(at >= half)
    def _():
        second[...] = value.astype(second.dtype)


def token_product(kernel, activs, weights, width, kinds):
    rows = 256
    total, hidden = activs[0].shape
    half = total // rows // 2
    return grid_call(
        kernel,
        2 * half,
        list(activs) + list(weights),
        [row_block(activ, rows) for activ in activs] + [whole_block(weight) for weight in weights],
        [jax.ShapeDtypeStruct((total // 2, width), kind) for kind in kinds],
        [
            pl.BlockSpec((rows, width), lambda at: (jnp.minimum(at, half - 1), 0)),
            pl.BlockSpec((rows, width), lambda at: (jnp.maximum(at - half, 0), 0)),
        ],
        10**9,
    )


def together(*values):
    return lax.optimization_barrier(values)


class Group:
    def __init__(self, size, replicas):
        self.size = size
        self.replicas = replicas
        self.at = lax.axis_index("fsdp")
        self.replica = lax.axis_index("rep")
        self.pair = size == 2 and replicas % 2 == 0

    def swap(self, value):
        return swapped(value, "fsdp", 0, 2)

    def fetched(self, rows, bits):
        start, count = 0, rows.shape[0]
        for bit in bits:
            count //= 2
            start = start + ((self.replica >> bit) & 1) * count
        return self.swap(lax.dynamic_slice_in_dim(rows, start, count, 0))

    def shared(self, part, bits):
        for bit in reversed(bits):
            other = swapped(part, "rep", bit, self.replicas)
            part = ordered(part, other, (self.replica >> bit) & 1)
            part = part.reshape((-1,) + part.shape[2:])
        return part

    def joined(self, own, other):
        return ordered(own, other, self.at).reshape((-1,) + own.shape[1:])

    def whole_vector(self, vector):
        if not self.pair:
            return lax.all_gather(vector, "fsdp", axis=0, tiled=False)
        return ordered(vector, self.swap(vector), self.at)

    def columns(self, rows, owner):
        width = rows.shape[1] // 2
        return lax.dynamic_slice_in_dim(rows, owner * width, width, 1)

    def plain_weights(self, qkv, w_output, w_gate, w_up):
        return (
            lax.all_gather(qkv, "fsdp", axis=0, tiled=True),
            lax.all_gather(w_output, "fsdp", axis=0, tiled=True),
            lax.all_to_all(w_gate, "fsdp", 1, 0, tiled=True),
            lax.all_to_all(w_up, "fsdp", 1, 0, tiled=True),
        )

    def all_tokens(self, value):
        return lax.all_gather(value, "fsdp", axis=0, tiled=True)

    def own_tokens(self, partial):
        return lax.psum_scatter(partial, "fsdp", scatter_dimension=0, tiled=True)

    def sum_parts(self, parts):
        if not self.pair:
            return lax.psum_scatter(parts, "fsdp", scatter_dimension=0, tiled=False)
        got = self.swap(chosen(parts, 1 - self.at))
        return added(chosen(parts, self.at), got)

    def exchange_parts(self, parts):
        if not self.pair:
            return lax.all_to_all(parts, "fsdp", 0, 0, tiled=True)
        got = self.swap(chosen(parts, 1 - self.at))
        return ordered(chosen(parts, self.at), got, self.at)


class Replicas:
    def __init__(self, size):
        self.size = size
        self.at = lax.axis_index("rep")
        self.bits = size.bit_length() - 1
        self.far = list(range(1, self.bits))

    def bit(self, bit):
        return (self.at >> bit) & 1

    def swap_core(self, value):
        return swapped(value, "rep", 0, self.size)

    def scatter(self, parts, bit):
        mine = self.bit(bit)
        got = swapped(chosen(parts, 1 - mine), "rep", bit, self.size)
        return added(chosen(parts, mine), got)

    def gather(self, value, bit):
        return ordered(value, swapped(value, "rep", bit, self.size), self.bit(bit))

    def first(self, parts, order):
        if not order:
            return parts
        return self.scatter(parts.reshape((2, -1) + parts.shape[1:]), order[0])

    def scatter_all(self, parts, order):
        for at in range(len(order)):
            parts = self.first(parts, order[at:])
        return parts.reshape(parts.shape[1:])

    def gather_all(self, value, order):
        value = value[None]
        for bit in reversed(order):
            value = self.gather(value, bit)
            value = value.reshape((value.shape[0] * value.shape[1],) + value.shape[2:])
        return value


def shards(
    tokens,
    segments,
    cotangent,
    w_query,
    w_key,
    w_value,
    w_output,
    w_gate,
    w_up,
    w_down,
    b_query,
    b_key,
    b_value,
    gain_attn,
    gain_mlp,
    group_size,
    replica_count,
):
    group = Group(group_size, replica_count)
    replicas = Replicas(replica_count)
    far = replicas.far
    near_first = [far[1], far[0]] + far[2:]
    eighth = 1 << len(far)
    width = tokens.shape[1]
    rows_own = w_query.shape[0]
    qw, kw = w_query.shape[1], w_key.shape[1]
    vectors = group.whole_vector(
        jnp.concatenate([b_query, b_key, b_value, gain_attn, gain_mlp])
    ).astype(jnp.float32)
    cuts = [0]
    for part in (b_query, b_key, b_value, gain_attn, gain_mlp):
        cuts.append(cuts[-1] + part.shape[0])
    bias_query, bias_key, bias_value, full_gain_attn, full_gain_mlp = (
        vectors[:, low:high].reshape(-1) for low, high in zip(cuts[:-1], cuts[1:])
    )
    qkv = jnp.concatenate([w_query, w_key, w_value], axis=1)
    live = (segments >= 0).astype(jnp.float32)[:, None]
    mlp_grad = (live * cotangent.astype(jnp.float32)).astype(jnp.bfloat16)
    cosine, sine = rope_tables(segments, HEAD_DIM)
    copies = LANES // HEAD_DIM
    cosine = jnp.concatenate([cosine, cosine] * copies, axis=1)
    sine = jnp.concatenate([-sine, sine] * copies, axis=1)
    segs_col, segs_row = segments[:, None], segments[None, :]
    normed_low = normed(tokens.astype(jnp.float32), full_gain_attn).astype(jnp.bfloat16)
    gain_attn_row, gain_mlp_row = full_gain_attn[None, :], full_gain_mlp[None, :]
    bias_row = jnp.concatenate([bias_query, bias_key, bias_value])[None, :]
    if group.pair:
        cores = [0]
        chips = [0, 1] if replica_count % 4 == 0 else [0]
        got_qkv, got_output = group.fetched(qkv, cores), group.fetched(w_output, cores)
        got_qkv, got_output, w_gate, w_up = together(got_qkv, got_output, w_gate, w_up)
        full_qkv = group.joined(qkv, group.shared(got_qkv, cores))
        full_output = group.joined(w_output, group.shared(got_output, cores))
        got_gate = group.fetched(group.columns(w_gate, 1 - group.at), chips)
        got_up = group.fetched(group.columns(w_up, 1 - group.at), chips)
    else:
        full_qkv, full_output, part_gate, part_up = group.plain_weights(
            qkv, w_output, w_gate, w_up
        )
    query_rot, key_rot, value_low, early = attention_early(
        normed_low, full_qkv, bias_row, cosine, sine, segs_col, segs_row, tokens, full_output,
        gain_mlp_row,
    )
    if group.pair:
        query_rot, early, got_gate, got_up, mlp_grad = together(
            query_rot, early, got_gate, got_up, mlp_grad
        )
        got_gate, got_up = group.shared(got_gate, chips[1:]), group.shared(got_up, chips[1:])
        others = [group.swap(early[3])]
        mlp_other = group.swap(mlp_grad)
    late = attention_late(
        query_rot, key_rot, value_low, segs_col, segs_row, tokens, full_output, gain_mlp_row
    )
    mid_own = jnp.concatenate([early[3], late[3]])
    length = tokens.shape[0]
    if group.pair:
        late, got_gate, got_up, others = together(late, got_gate, got_up, others)
        others.append(group.swap(late[3]))
        got_gate, got_up = group.shared(got_gate, cores), group.shared(got_up, cores)
        part_gate = group.joined(group.columns(w_gate, group.at), got_gate)
        part_up = group.joined(group.columns(w_up, group.at), got_up)
        hidden = hidden_part(
            mid_own, mlp_grad, part_gate, part_up, w_down, group_size * length, 0, ()
        )
        hidden, others, mlp_other = together(hidden, others, mlp_other)
        mid_other = jnp.concatenate(others)
        activ_low, gate_grad, up_grad = hidden_part(
            mid_other, mlp_other, part_gate, part_up, w_down, group_size * length, length, hidden
        )
        mid_all = jnp.concatenate([mid_own, mid_other])
        mlp_grad_all = jnp.concatenate([mlp_grad, mlp_other])
    else:
        mid_all = group.all_tokens(mid_own)
        mlp_grad_all = group.all_tokens(mlp_grad)
        activ_low, gate_grad, up_grad = hidden_part(
            mid_all, mlp_grad_all, part_gate, part_up, w_down, group_size * length, 0, ()
        )
    middle = jnp.concatenate([early[2], late[2]])

    back_weights, out_weights = (part_gate, part_up), (w_down,)
    back = (gate_grad, up_grad)
    kinds = (jnp.float32, jnp.bfloat16) if group.pair else (jnp.float32, jnp.float32)
    norm_own, norm_other = token_product(norm_part_kernel, back, back_weights, width, kinds)
    norm_own, norm_other, activ_low, back = together(norm_own, norm_other, activ_low, back)
    grad_down = contract_rows(activ_low, mlp_grad_all).astype(jnp.bfloat16)
    grad_down, back = together(grad_down, back)
    gate_grad, up_grad = back
    grad_gate = contract_rows(mid_all, gate_grad).astype(jnp.bfloat16)
    grad_up = contract_rows(mid_all, up_grad).astype(jnp.bfloat16)
    down = replicas.scatter(grad_down.reshape(2, -1, width), 0).reshape(eighth, -1, width)
    grad_gate, grad_up, down, back, activ_low = together(
        grad_gate, grad_up, down, back, activ_low
    )
    hidden_units = grad_gate.shape[1]
    cut = -(-hidden_units // 256) * 128
    core = replicas.bit(0)
    pair_parts = []
    for low, high in ((0, cut), (cut, hidden_units)):
        gate_range, up_range = grad_gate[:, low:high], grad_up[:, low:high]
        got = replicas.swap_core(jnp.where(core == 0, up_range, gate_range))
        summed = added(jnp.where(core == 0, gate_range, up_range), got)
        summed = summed.reshape(group_size, eighth, rows_own // eighth, high - low)
        pair_parts.append(summed.transpose(1, 0, 2, 3))
    first, second = pair_parts
    down = replicas.first(down, far)
    out_own, out_other = token_product(
        out_part_kernel, (activ_low,), out_weights, width, kinds
    )
    if group.pair:
        norm_got = group.swap(norm_other)
    else:
        norm_own = group.own_tokens(jnp.concatenate([norm_own, norm_other]))
        norm_got = jnp.zeros((length, width), jnp.bfloat16)
    norm_own, norm_got, out_own, out_other, down, first, second = together(
        norm_own, norm_got, out_own, out_other, down, first, second
    )
    columns = full_qkv.shape[1] + width
    unit = 16 * eighth
    padded = -(-(rows_own + 16) // unit) * unit
    attn, input_grad = attention_backward(
        group_size, padded, early, late, norm_own, norm_got, cotangent, gain_mlp_row, full_output,
        query_rot, key_rot, value_low, segs_col, segs_row, cosine, sine, normed_low, full_qkv,
        tokens, gain_attn_row,
    )
    down = replicas.first(down, far[1:])
    first = replicas.first(first, near_first)
    second = replicas.first(second, far)
    if group.pair:
        out_sum = out_own + group.swap(out_other).astype(jnp.float32)
    else:
        out_sum = group.own_tokens(jnp.concatenate([out_own, out_other]))
    attn, down, first, second = together(attn, down, first, second)
    output = (middle + live * out_sum).astype(jnp.bfloat16)
    attn = replicas.scatter(
        attn.reshape(group_size, 2, padded // 2, columns).transpose(1, 0, 2, 3), 0
    )
    attn = group.sum_parts(attn).reshape(eighth, -1, columns)
    attn = replicas.scatter_all(attn, near_first)
    down = replicas.scatter_all(down, far[2:])
    first = group.exchange_parts(replicas.scatter_all(first, near_first[1:]))
    second = group.exchange_parts(replicas.scatter_all(second, far[1:]))
    down = replicas.gather(replicas.gather_all(down, far), 0)
    first = replicas.gather_all(first, near_first)
    second = replicas.gather_all(second, far)
    attn = replicas.gather_all(attn, near_first)
    shard_down = down.reshape(-1, width).astype(jnp.float32)
    gate_parts = [[] for _ in range(group_size)]
    up_parts = [[] for _ in range(group_size)]
    for mine in (first, second):
        got = replicas.swap_core(mine)
        for matrix, parts in (
            (jnp.where(core == 0, mine, got), gate_parts),
            (jnp.where(core == 0, got, mine), up_parts),
        ):
            for sender in range(group_size):
                parts[sender].append(matrix[:, sender].reshape(rows_own, -1))
    shard_gate, shard_up = (
        jnp.concatenate(sum(parts, []), axis=1).astype(jnp.float32)
        for parts in (gate_parts, up_parts)
    )
    attn_sum = replicas.gather(attn, 0).reshape(padded, columns).astype(jnp.float32)
    shard_query = attn_sum[:rows_own, :qw]
    shard_key = attn_sum[:rows_own, qw : qw + kw]
    shard_value = attn_sum[:rows_own, qw + kw : qw + 2 * kw]
    shard_output = attn_sum[:rows_own, qw + 2 * kw :]
    bias_sum = attn_sum[rows_own, : columns - width]
    shard_vectors = tuple(
        chosen(vector.reshape(group_size, -1), group.at)
        for vector in (
            bias_sum[:qw],
            bias_sum[qw : qw + kw],
            bias_sum[qw + kw :],
            attn_sum[rows_own, columns - width :],
            attn_sum[rows_own + 1, :width],
        )
    )
    return (
        output,
        input_grad,
        shard_query,
        shard_key,
        shard_value,
        shard_output,
        shard_gate,
        shard_up,
        shard_down,
    ) + shard_vectors


def solution(mesh):
    placed = (
        P(("rep", "fsdp"), None),
        P(("rep", "fsdp")),
        P(("rep", "fsdp"), None),
        P("fsdp", None),
        P("fsdp", None),
        P("fsdp", None),
        P("fsdp", None),
        P("fsdp", None),
        P("fsdp", None),
        P("fsdp", None),
        P("fsdp"),
        P("fsdp"),
        P("fsdp"),
        P("fsdp"),
        P("fsdp"),
    )
    return jax.shard_map(
        functools.partial(
            shards, group_size=mesh.shape["fsdp"], replica_count=mesh.shape["rep"]
        ),
        mesh=mesh,
        in_specs=placed,
        out_specs=(
            P(("rep", "fsdp"), None),
            P(("rep", "fsdp"), None),
            P("fsdp", None),
            P("fsdp", None),
            P("fsdp", None),
            P("fsdp", None),
            P("fsdp", None),
            P("fsdp", None),
            P("fsdp", None),
            P("fsdp"),
            P("fsdp"),
            P("fsdp"),
            P("fsdp"),
            P("fsdp"),
        ),
        check_vma=False,
    )
```

```python
import functools

import jax
import jax.numpy as jnp
from jax import lax
from jax.experimental import pallas as pl
from jax.experimental.pallas import tpu as pltpu
from jax.sharding import PartitionSpec as P

HEAD_DIM = 64


EPSILON = 1e-06
THETA = 1000000.0
NEGATIVE = -1e30


def positions(segs):
    length = segs.shape[0]
    index = jnp.arange(length, dtype=jnp.int32)
    before = jnp.concatenate([jnp.full((1,), -2, dtype=jnp.int32), segs[:-1]])
    starts = lax.cummax(jnp.where(segs != before, index, jnp.zeros_like(index)), axis=0)
    return (index - starts).astype(jnp.float32)


def rope_tables(segs, head_dim):
    halfway = head_dim // 2
    inverse = THETA ** (-(jnp.arange(halfway, dtype=jnp.float32) * 2.0 / head_dim))
    angles = positions(segs)[:, None] * inverse[None, :]
    return (jnp.cos(angles), jnp.sin(angles))


def normed(values, gain):
    scale = lax.rsqrt(jnp.mean(values * values, axis=-1, keepdims=True) + EPSILON)
    return values * scale * gain


def forward_product(left, right):
    return jnp.dot(left, right, preferred_element_type=jnp.float32)


def contract_rows(left, right):
    return lax.dot_general(
        left, right, (((0,), (0,)), ((), ())), preferred_element_type=jnp.float32
    )


def contract_cols(left, right):
    return lax.dot_general(
        left, right, (((1,), (1,)), ((), ())), preferred_element_type=jnp.float32
    )


LANES = 128


def lane_index(shape):
    return lax.broadcasted_iota(jnp.int32, shape, len(shape) - 1)


def swapped_halves(values):
    half = HEAD_DIM // 2
    lanes = lane_index(values.shape)
    return jnp.where(
        lanes % HEAD_DIM < half,
        pltpu.roll(values, LANES - half, 1),
        pltpu.roll(values, half, 1),
    )


def doubled(pair, head):
    lanes = lane_index(pair.shape)
    wide = pair.astype(jnp.float32)
    other = pltpu.roll(wide, HEAD_DIM, 1)
    return jnp.where((lanes < HEAD_DIM) == (head == 0), wide, other).astype(jnp.bfloat16)


def one_head(pair, parity):
    lanes = lane_index(pair.shape)
    return jnp.where((lanes < HEAD_DIM) == (parity == 0), pair, jnp.zeros_like(pair))


def mask_bias(key_segs, row_segs, row_start):
    keys, rows = key_segs.shape[0], row_segs.shape[1]
    key_index = lax.broadcasted_iota(jnp.int32, (keys, rows), 0)
    row_index = row_start + lax.broadcasted_iota(jnp.int32, (keys, rows), 1)
    allowed = (key_segs == row_segs) & (row_index >= key_index)
    return jnp.where(allowed, 0.0, NEGATIVE).astype(jnp.float32)


def is_live(segs):
    return jnp.where(segs >= 0, 1.0, 0.0)


def turned_over(values):
    return jnp.transpose(values.astype(jnp.float32)).astype(jnp.bfloat16)


def one_of_pair(first, second):
    rows = lax.broadcasted_iota(jnp.int32, first.shape, 0)
    return jnp.where(rows < HEAD_DIM, first, second)


def attend_rows(
    row_start, key_count, groups, pairs, segs_col, segs_row, query_rot, key_rot, value_low,
    bias, keys_two, values_over, attended, logs, tokens, w_output, gain, middle, mid_low,
):
    rows = attended.shape[0]
    for kv_head in range(2):
        keys_two[kv_head] = doubled(key_rot[:key_count, :], kv_head)
        values_over[kv_head] = turned_over(doubled(value_low[:key_count, :], kv_head))
    bias[...] = mask_bias(
        segs_col[:key_count], segs_row[:, row_start : row_start + rows], row_start
    )

    def one_pair(pair, carry):
        cols = pl.ds(pl.multiple_of(pair * LANES, LANES), LANES)
        queries = query_rot[row_start : row_start + rows, cols]
        results = []
        for parity in range(2):
            head = 2 * pair + parity
            kv_head = head // groups
            query = one_head(queries, parity) * jnp.asarray(HEAD_DIM**-0.5, jnp.bfloat16)
            scores = contract_cols(keys_two[kv_head], query) + bias[...]
            row_max = jnp.max(scores, axis=0, keepdims=True)
            exponent = jnp.exp(scores - row_max)
            row_total = jnp.sum(exponent, axis=0, keepdims=True)
            probs = (exponent * (1.0 / row_total)).astype(jnp.bfloat16)
            results.append(forward_product(values_over[kv_head], probs))
            logs[pl.ds(head, 1), :] = row_max + jnp.log(row_total)
        attended[:, cols] = jnp.transpose(one_of_pair(*results)).astype(jnp.bfloat16)
        return carry

    lax.fori_loop(0, pairs, one_pair, 0)
    mixed = forward_product(attended[...], w_output[...])
    here = slice(row_start, row_start + rows)
    total = tokens[here, :].astype(jnp.float32) + is_live(segs_col[here, :]) * mixed
    middle[...] = total
    mid_low[...] = normed(total, gain[...]).astype(jnp.bfloat16)


def early_kernel(
    groups, pairs, normed_low, w_qkv, bias_qkv, cosine, sine, segs_col, segs_row, tokens,
    w_output, gain, query_rot, key_rot, value_low, attended, logs, middle, mid_low,
    bias, keys_two, values_over,
):
    def project(pair):
        cols = pl.ds(pl.multiple_of(pair * LANES, LANES), LANES)
        return forward_product(normed_low[...], w_qkv[:, cols]) + bias_qkv[:, cols]

    def turned(values):
        return (values * cosine[...] + swapped_halves(values) * sine[...]).astype(jnp.bfloat16)

    def query_pair(pair, carry):
        cols = pl.ds(pl.multiple_of(pair * LANES, LANES), LANES)
        query_rot[:, cols] = turned(project(pair))
        return carry

    lax.fori_loop(0, pairs, query_pair, 0)
    key_rot[...] = turned(project(pairs))
    value_low[...] = project(pairs + 1).astype(jnp.bfloat16)
    attend_rows(
        0, attended.shape[0], groups, pairs, segs_col, segs_row, query_rot, key_rot, value_low,
        bias, keys_two, values_over, attended, logs, tokens, w_output, gain, middle, mid_low,
    )


def late_kernel(
    groups, pairs, query_rot, key_rot, value_low, segs_col, segs_row, tokens,
    w_output, gain, attended, logs, middle, mid_low, bias, keys_two, values_over,
):
    rows = attended.shape[0]
    attend_rows(
        rows, 2 * rows, groups, pairs, segs_col, segs_row, query_rot, key_rot, value_low,
        bias, keys_two, values_over, attended, logs, tokens, w_output, gain, middle, mid_low,
    )


def call(kernel, out_shape, scratch, cost, operands):
    return pl.pallas_call(
        kernel,
        out_shape=[jax.ShapeDtypeStruct(shape, kind) for shape, kind in out_shape],
        in_specs=[pl.BlockSpec(memory_space=pltpu.VMEM)] * len(operands),
        out_specs=[pl.BlockSpec(memory_space=pltpu.VMEM)] * len(out_shape),
        scratch_shapes=[pltpu.VMEM(shape, kind) for shape, kind in scratch],
        compiler_params=pltpu.CompilerParams(vmem_limit_bytes=56 * 2**20),
        cost_estimate=pl.CostEstimate(flops=cost, bytes_accessed=cost // 300, transcendentals=0),
    )(*operands)


def attention_shapes(length, key_count, w_output, kw):
    queries, width = w_output.shape
    rows = length // 2
    heads = -(-queries // HEAD_DIM // 8) * 8
    low, wide = jnp.bfloat16, jnp.float32
    half_out = [
        ((rows, queries), low), ((heads, rows), wide), ((rows, width), wide), ((rows, width), low)
    ]
    scratch = [
        ((key_count, rows), wide), ((2, key_count, LANES), low), ((2, LANES, key_count), low)
    ]
    return queries, queries // kw, queries // LANES, half_out, scratch


def attention_early(
    normed_low, w_qkv, bias_qkv, cosine, sine, segs_col, segs_row, tokens, w_output, gain
):
    length = tokens.shape[0]
    kw = (w_qkv.shape[1] - w_output.shape[0]) // 2
    queries, groups, pairs, half_out, scratch = attention_shapes(
        length, length // 2, w_output, kw
    )
    whole = [((length, columns), jnp.bfloat16) for columns in (queries, kw, kw)]
    query_rot, key_rot, value_low, *early = call(
        functools.partial(early_kernel, groups, pairs),
        whole + half_out,
        scratch,
        10**6,
        (normed_low, w_qkv, bias_qkv, cosine, sine, segs_col, segs_row, tokens, w_output, gain),
    )
    return query_rot, key_rot, value_low, early


def attention_late(query_rot, key_rot, value_low, segs_col, segs_row, tokens, w_output, gain):
    length = tokens.shape[0]
    _, groups, pairs, half_out, scratch = attention_shapes(
        length, length, w_output, key_rot.shape[1]
    )
    return call(
        functools.partial(late_kernel, groups, pairs),
        half_out,
        scratch,
        10**6,
        (query_rot, key_rot, value_low, segs_col, segs_row, tokens, w_output, gain),
    )


def norm_pull(values, gain, grad):
    scale = lax.rsqrt(jnp.mean(values * values, axis=-1, keepdims=True) + EPSILON)
    unit = values * scale
    inner = grad * gain
    pull = scale * (inner - unit * jnp.mean(inner * unit, axis=-1, keepdims=True))
    return pull, jnp.sum(grad * unit, axis=0, keepdims=True)


def backward_kernel(
    groups, pairs, devices, mid_early, mid_late, norm_own, norm_got, cotangent, gain_mlp, w_output,
    att_early, att_late, log_early, log_late, query_rot, key_rot, value_low, segs_col, segs_row,
    cosine, sine, normed_low, w_qkv, tokens, gain_attn,
    sums, input_grad, attn_grad, attended_grad, low_grads, bias, keys_two, keys_over, values_two, key_grad, value_grad,
    qkv_sums, out_sums,
):
    rows = mid_early.shape[0]
    length = 2 * rows
    parts = ((0, mid_early, att_early, log_early), (rows, mid_late, att_late, log_late))
    width, columns = w_qkv.shape
    own = width // devices
    padded = sums.shape[0] // devices

    def sum_row(row, first, value):
        low = value.astype(jnp.bfloat16)
        for device in range(devices):
            at = device * padded + own + row
            sums[at : at + 1, first : first + low.shape[1]] = low

    for device in range(devices):
        at = device * padded + own
        sums[at : at + padded - own, :] = jnp.zeros((padded - own, sums.shape[1]), jnp.bfloat16)
    gain_sum = jnp.zeros(gain_mlp.shape, jnp.float32)
    for start, middle, _, _ in parts:
        here = slice(start, start + rows)
        pull, gain_part = norm_pull(
            middle[...],
            gain_mlp[...],
            norm_own[here, :] + norm_got[here, :].astype(jnp.float32),
        )
        gain_sum = gain_sum + gain_part
        total = cotangent[here, :].astype(jnp.float32) + pull
        input_grad[here, :] = total
        attn_grad[here, :] = (is_live(segs_col[here, :]) * total).astype(jnp.bfloat16)
        bias[: start + rows, here] = mask_bias(segs_col[: start + rows], segs_row[:, here], start)
    sum_row(1, 0, gain_sum)
    for kv_head in range(2):
        keys_two[kv_head] = doubled(key_rot[...], kv_head)
        keys_over[kv_head] = turned_over(keys_two[kv_head])
        values_two[kv_head] = doubled(value_low[...], kv_head)
    key_grad[...] = jnp.zeros_like(key_grad)
    value_grad[...] = jnp.zeros_like(value_grad)
    for start in range(0, length, rows):
        here = slice(start, start + rows)
        attended_grad[here, :] = contract_cols(attn_grad[here, :], w_output[...]).astype(
            jnp.bfloat16
        )

    def turned_back(values, here):
        return values * cosine[here, :] - swapped_halves(values) * sine[here, :]

    def one_pair(pair, carry):
        cols = pl.ds(pl.multiple_of(pair * LANES, LANES), LANES)
        out_grad = jnp.zeros((LANES, attn_grad.shape[1]), jnp.float32)
        for start, _, attended, logs in parts:
            here = slice(start, start + rows)
            keys = start + rows
            out_grad = out_grad + contract_rows(attended[:, cols], attn_grad[here, :])
            queries = query_rot[here, cols]
            grads = attended_grad[here, cols]
            results = []
            for parity in range(2):
                head = 2 * pair + parity
                kv_head = head // groups
                query = one_head(queries, parity) * jnp.asarray(HEAD_DIM**-0.5, jnp.bfloat16)
                grad = one_head(grads, parity)
                scores = contract_cols(keys_two[kv_head, :keys], query) + bias[:keys, here]
                probs = jnp.exp(scores - logs[pl.ds(head, 1), :])
                prob_grad = contract_cols(values_two[kv_head, :keys], grad)
                inner = jnp.sum(prob_grad * probs, axis=0, keepdims=True)
                score_grad = (probs * (prob_grad - inner)).astype(jnp.bfloat16)
                value_grad[kv_head, :keys] += forward_product(probs.astype(jnp.bfloat16), grad)
                key_grad[kv_head, :keys] += forward_product(score_grad, query)
                results.append(forward_product(keys_over[kv_head, :, :keys], score_grad))
            query_grad = jnp.transpose(one_of_pair(*results)) * HEAD_DIM**-0.5
            low = turned_back(query_grad, here).astype(jnp.bfloat16)
            low_grads[here, cols] = low
        out_sums[cols, :] = out_grad.astype(jnp.bfloat16)
        return carry

    lax.fori_loop(0, pairs, one_pair, 0)

    def folded(pair_sums):
        both = [pair_sums[at] + pltpu.roll(pair_sums[at], HEAD_DIM, 1) for at in range(2)]
        return jnp.where(lane_index(both[0].shape) < HEAD_DIM, both[0], both[1])

    everywhere = slice(0, length)
    key_low = turned_back(folded(key_grad), everywhere).astype(jnp.bfloat16)
    value_grad_low = folded(value_grad).astype(jnp.bfloat16)
    for at, low in ((pairs, key_low), (pairs + 1, value_grad_low)):
        cols = slice(at * LANES, (at + 1) * LANES)
        low_grads[:, cols] = low
    sum_row(0, 0, jnp.sum(low_grads[...].astype(jnp.float32), axis=0, keepdims=True))

    def weight_rows(block, carry):
        cols = pl.ds(pl.multiple_of(block * LANES, LANES), LANES)
        qkv_sums[cols, :] = contract_rows(normed_low[:, cols], low_grads[...]).astype(jnp.bfloat16)
        return carry

    lax.fori_loop(0, width // LANES, weight_rows, 0)
    for device in range(devices):
        here = slice(device * padded, device * padded + own)
        there = slice(device * own, (device + 1) * own)
        sums[here, :columns] = qkv_sums[there, :]
        sums[here, columns:] = out_sums[there, :]
    gain_sum = jnp.zeros(gain_attn.shape, jnp.float32)
    for start in range(0, length, rows):
        here = slice(start, start + rows)
        norm_in = contract_cols(low_grads[here, :], w_qkv[...])
        pull, gain_part = norm_pull(tokens[here, :].astype(jnp.float32), gain_attn[...], norm_in)
        gain_sum = gain_sum + gain_part
        input_grad[here, :] += pull
    sum_row(0, columns, gain_sum)


def attention_backward(
    devices, padded, early, late, norm_own, norm_got, cotangent, gain_mlp, w_output, query_rot, key_rot, value_low,
    segs_col, segs_row, cosine, sine, normed_low, w_qkv, tokens, gain_attn,
):
    length, width = tokens.shape
    queries = w_output.shape[0]
    columns = w_qkv.shape[1]
    kw = (columns - queries) // 2
    low, wide = jnp.bfloat16, jnp.float32
    return call(
        functools.partial(backward_kernel, queries // kw, queries // LANES, devices),
        [((devices * padded, columns + width), low), ((length, width), wide)],
        [
            ((length, width), low),
            ((length, queries), low),
            ((length, columns), low),
            ((length, length), wide),
            ((2, length, LANES), low),
            ((2, LANES, length), low),
            ((2, length, LANES), low),
            ((2, length, LANES), wide),
            ((2, length, LANES), wide),
            ((width, columns), low),
            ((queries, width), low),
        ],
        10**6,
        (early[2], late[2], norm_own, norm_got, cotangent, gain_mlp, w_output, early[0], late[0],
         early[1], late[1], query_rot, key_rot, value_low, segs_col, segs_row, cosine, sine,
         normed_low, w_qkv, tokens, gain_attn),
    )


def swapped(value, axis, bit, size):
    step = 1 << bit
    return lax.ppermute(value, axis, [(at, at ^ step) for at in range(size)])


def chosen(parts, at):
    return lax.dynamic_index_in_dim(parts, at, 0, keepdims=False)


def added(left, right):
    return (left.astype(jnp.float32) + right.astype(jnp.float32)).astype(jnp.bfloat16)


def ordered(own, other, bit):
    return jnp.where(bit == 0, jnp.stack([own, other]), jnp.stack([other, own]))


def column_cuts(columns):
    step = 4 * LANES
    return [(low, min(low + step, columns)) for low in range(0, columns, step)]


def hidden_kernel(carries, mid_low, mlp_grad, w_gate, w_up, w_down, *refs):
    activ, gate_grad, up_grad = refs[carries:]
    for low, high in column_cuts(w_gate.shape[1]):
        gate = forward_product(mid_low[...], w_gate[:, low:high])
        upward = forward_product(mid_low[...], w_up[:, low:high])
        grad = contract_cols(mlp_grad[...], w_down[low:high, :])
        sigmoid = jax.nn.sigmoid(gate)
        silu = gate * sigmoid
        activ[:, low:high] = (silu * upward).astype(jnp.bfloat16)
        gate_grad[:, low:high] = (grad * upward * (sigmoid + silu * (1.0 - sigmoid))).astype(
            jnp.bfloat16
        )
        up_grad[:, low:high] = (grad * silu).astype(jnp.bfloat16)


def whole_block(array):
    return pl.BlockSpec(array.shape, lambda at: (0,) * array.ndim)


def row_block(array, rows, start=0):
    return pl.BlockSpec((rows, array.shape[1]), lambda at: (at + start, 0))


def grid_call(kernel, grid, operands, in_specs, out_shape, out_specs, flops, aliases=None):
    return pl.pallas_call(
        kernel,
        grid=(grid,),
        out_shape=out_shape,
        in_specs=in_specs,
        out_specs=out_specs,
        input_output_aliases=aliases or {},
        compiler_params=pltpu.CompilerParams(vmem_limit_bytes=56 * 2**20),
        cost_estimate=pl.CostEstimate(flops=flops, bytes_accessed=10**3, transcendentals=0),
    )(*operands)


def hidden_part(mid_low, mlp_grad, w_gate, w_up, w_down, total, start, carried):
    rows = 256
    count = mid_low.shape[0] // rows
    first = start // rows
    shapes = [jax.ShapeDtypeStruct((total, w_gate.shape[1]), jnp.bfloat16)] * 3
    return grid_call(
        functools.partial(hidden_kernel, len(carried)),
        count,
        [mid_low, mlp_grad, w_gate, w_up, w_down] + list(carried),
        [row_block(mid_low, rows), row_block(mlp_grad, rows)]
        + [whole_block(weight) for weight in (w_gate, w_up, w_down)]
        + [pl.BlockSpec(memory_space=pl.ANY)] * len(carried),
        shapes,
        [row_block(shape, rows, first) for shape in shapes],
        10**6,
        {5 + at: at for at in range(len(carried))},
    )


def norm_part_kernel(gate_grad, up_grad, w_gate, w_up, first, second):
    value = contract_cols(gate_grad[...], w_gate[...]) + contract_cols(up_grad[...], w_up[...])
    two_parts(value, first, second)


def out_part_kernel(activ, w_down, first, second):
    two_parts(forward_product(activ[...], w_down[...]), first, second)


def two_parts(value, first, second):
    at, half = pl.program_id(0), pl.num_programs(0) // 2

    @pl.when(at < half)
    def _():
        first[...] = value.astype(first.dtype)

    @pl.when(at >= half)
    def _():
        second[...] = value.astype(second.dtype)


def token_product(kernel, activs, weights, width, kinds):
    rows = 256
    total, hidden = activs[0].shape
    half = total // rows // 2
    return grid_call(
        kernel,
        2 * half,
        list(activs) + list(weights),
        [row_block(activ, rows) for activ in activs] + [whole_block(weight) for weight in weights],
        [jax.ShapeDtypeStruct((total // 2, width), kind) for kind in kinds],
        [
            pl.BlockSpec((rows, width), lambda at: (jnp.minimum(at, half - 1), 0)),
            pl.BlockSpec((rows, width), lambda at: (jnp.maximum(at - half, 0), 0)),
        ],
        10**6,
    )


def together(*values):
    return lax.optimization_barrier(values)


class Group:
    def __init__(self, size, replicas):
        self.size = size
        self.replicas = replicas
        self.at = lax.axis_index("fsdp")
        self.replica = lax.axis_index("rep")
        self.pair = size == 2 and replicas % 2 == 0

    def swap(self, value):
        return swapped(value, "fsdp", 0, 2)

    def fetched(self, rows, bits):
        start, count = 0, rows.shape[0]
        for bit in bits:
            count //= 2
            start = start + ((self.replica >> bit) & 1) * count
        return self.swap(lax.dynamic_slice_in_dim(rows, start, count, 0))

    def shared(self, part, bits):
        for bit in reversed(bits):
            other = swapped(part, "rep", bit, self.replicas)
            part = ordered(part, other, (self.replica >> bit) & 1)
            part = part.reshape((-1,) + part.shape[2:])
        return part

    def joined(self, own, other):
        return ordered(own, other, self.at).reshape((-1,) + own.shape[1:])

    def whole_vector(self, vector):
        if not self.pair:
            return lax.all_gather(vector, "fsdp", axis=0, tiled=False)
        return ordered(vector, self.swap(vector), self.at)

    def columns(self, rows, owner):
        width = rows.shape[1] // 2
        return lax.dynamic_slice_in_dim(rows, owner * width, width, 1)

    def plain_weights(self, qkv, w_output, w_gate, w_up):
        return (
            lax.all_gather(qkv, "fsdp", axis=0, tiled=True),
            lax.all_gather(w_output, "fsdp", axis=0, tiled=True),
            lax.all_to_all(w_gate, "fsdp", 1, 0, tiled=True),
            lax.all_to_all(w_up, "fsdp", 1, 0, tiled=True),
        )

    def all_tokens(self, value):
        return lax.all_gather(value, "fsdp", axis=0, tiled=True)

    def own_tokens(self, partial):
        return lax.psum_scatter(partial, "fsdp", scatter_dimension=0, tiled=True)

    def sum_parts(self, parts):
        if not self.pair:
            return lax.psum_scatter(parts, "fsdp", scatter_dimension=0, tiled=False)
        got = self.swap(chosen(parts, 1 - self.at))
        return added(chosen(parts, self.at), got)

    def exchange_parts(self, parts):
        if not self.pair:
            return lax.all_to_all(parts, "fsdp", 0, 0, tiled=True)
        got = self.swap(chosen(parts, 1 - self.at))
        return ordered(chosen(parts, self.at), got, self.at)


class Replicas:
    def __init__(self, size):
        self.size = size
        self.at = lax.axis_index("rep")
        self.bits = size.bit_length() - 1
        self.far = list(range(1, self.bits))

    def bit(self, bit):
        return (self.at >> bit) & 1

    def swap_core(self, value):
        return swapped(value, "rep", 0, self.size)

    def scatter(self, parts, bit):
        mine = self.bit(bit)
        got = swapped(chosen(parts, 1 - mine), "rep", bit, self.size)
        return added(chosen(parts, mine), got)

    def gather(self, value, bit):
        return ordered(value, swapped(value, "rep", bit, self.size), self.bit(bit))

    def first(self, parts, order):
        if not order:
            return parts
        return self.scatter(parts.reshape((2, -1) + parts.shape[1:]), order[0])

    def scatter_all(self, parts, order):
        for at in range(len(order)):
            parts = self.first(parts, order[at:])
        return parts.reshape(parts.shape[1:])

    def gather_all(self, value, order):
        value = value[None]
        for bit in reversed(order):
            value = self.gather(value, bit)
            value = value.reshape((value.shape[0] * value.shape[1],) + value.shape[2:])
        return value


def shards(
    tokens,
    segments,
    cotangent,
    w_query,
    w_key,
    w_value,
    w_output,
    w_gate,
    w_up,
    w_down,
    b_query,
    b_key,
    b_value,
    gain_attn,
    gain_mlp,
    group_size,
    replica_count,
):
    group = Group(group_size, replica_count)
    replicas = Replicas(replica_count)
    far = replicas.far
    near_first = [far[1], far[0]] + far[2:]
    eighth = 1 << len(far)
    width = tokens.shape[1]
    rows_own = w_query.shape[0]
    qw, kw = w_query.shape[1], w_key.shape[1]
    vectors = group.whole_vector(
        jnp.concatenate([b_query, b_key, b_value, gain_attn, gain_mlp])
    ).astype(jnp.float32)
    cuts = [0]
    for part in (b_query, b_key, b_value, gain_attn, gain_mlp):
        cuts.append(cuts[-1] + part.shape[0])
    bias_query, bias_key, bias_value, full_gain_attn, full_gain_mlp = (
        vectors[:, low:high].reshape(-1) for low, high in zip(cuts[:-1], cuts[1:])
    )
    qkv = jnp.concatenate([w_query, w_key, w_value], axis=1)
    live = (segments >= 0).astype(jnp.float32)[:, None]
    mlp_grad = (live * cotangent.astype(jnp.float32)).astype(jnp.bfloat16)
    cosine, sine = rope_tables(segments, HEAD_DIM)
    copies = LANES // HEAD_DIM
    cosine = jnp.concatenate([cosine, cosine] * copies, axis=1)
    sine = jnp.concatenate([-sine, sine] * copies, axis=1)
    segs_col, segs_row = segments[:, None], segments[None, :]
    normed_low = normed(tokens.astype(jnp.float32), full_gain_attn).astype(jnp.bfloat16)
    gain_attn_row, gain_mlp_row = full_gain_attn[None, :], full_gain_mlp[None, :]
    bias_row = jnp.concatenate([bias_query, bias_key, bias_value])[None, :]
    if group.pair:
        cores = [0]
        chips = [0, 1] if replica_count % 4 == 0 else [0]
        got_qkv, got_output = group.fetched(qkv, cores), group.fetched(w_output, cores)
        got_qkv, got_output, w_gate, w_up = together(got_qkv, got_output, w_gate, w_up)
        full_qkv = group.joined(qkv, group.shared(got_qkv, cores))
        full_output = group.joined(w_output, group.shared(got_output, cores))
        got_gate = group.fetched(group.columns(w_gate, 1 - group.at), chips)
        got_up = group.fetched(group.columns(w_up, 1 - group.at), cores)
    else:
        full_qkv, full_output, part_gate, part_up = group.plain_weights(
            qkv, w_output, w_gate, w_up
        )
    query_rot, key_rot, value_low, early = attention_early(
        normed_low, full_qkv, bias_row, cosine, sine, segs_col, segs_row, tokens, full_output,
        gain_mlp_row,
    )
    if group.pair:
        query_rot, early, got_gate, mlp_grad = together(query_rot, early, got_gate, mlp_grad)
        got_gate = group.shared(got_gate, chips[1:])
        others = [group.swap(early[3])]
        mlp_other = group.swap(mlp_grad)
    late = attention_late(
        query_rot, key_rot, value_low, segs_col, segs_row, tokens, full_output, gain_mlp_row
    )
    mid_own = jnp.concatenate([early[3], late[3]])
    length = tokens.shape[0]
    if group.pair:
        late, got_gate, got_up, others = together(late, got_gate, got_up, others)
        others.append(group.swap(late[3]))
        got_gate, got_up = group.shared(got_gate, cores), group.shared(got_up, cores)
        part_gate = group.joined(group.columns(w_gate, group.at), got_gate)
        part_up = group.joined(group.columns(w_up, group.at), got_up)
        hidden = hidden_part(
            mid_own, mlp_grad, part_gate, part_up, w_down, group_size * length, 0, ()
        )
        hidden, others, mlp_other = together(hidden, others, mlp_other)
        mid_other = jnp.concatenate(others)
        activ_low, gate_grad, up_grad = hidden_part(
            mid_other, mlp_other, part_gate, part_up, w_down, group_size * length, length, hidden
        )
        mid_all = jnp.concatenate([mid_own, mid_other])
        mlp_grad_all = jnp.concatenate([mlp_grad, mlp_other])
    else:
        mid_all = group.all_tokens(mid_own)
        mlp_grad_all = group.all_tokens(mlp_grad)
        activ_low, gate_grad, up_grad = hidden_part(
            mid_all, mlp_grad_all, part_gate, part_up, w_down, group_size * length, 0, ()
        )
    middle = jnp.concatenate([early[2], late[2]])

    back_weights, out_weights = (part_gate, part_up), (w_down,)
    back = (gate_grad, up_grad)
    kinds = (jnp.float32, jnp.bfloat16) if group.pair else (jnp.float32, jnp.float32)
    norm_own, norm_other = token_product(norm_part_kernel, back, back_weights, width, kinds)
    norm_own, norm_other, activ_low, back = together(norm_own, norm_other, activ_low, back)
    grad_down = contract_rows(activ_low, mlp_grad_all).astype(jnp.bfloat16)
    grad_down, back = together(grad_down, back)
    gate_grad, up_grad = back
    grad_gate = contract_rows(mid_all, gate_grad).astype(jnp.bfloat16)
    grad_up = contract_rows(mid_all, up_grad).astype(jnp.bfloat16)
    down = replicas.scatter(grad_down.reshape(2, -1, width), 0).reshape(eighth, -1, width)
    grad_gate, grad_up, down, back, activ_low = together(
        grad_gate, grad_up, down, back, activ_low
    )
    hidden_units = grad_gate.shape[1]
    cut = -(-hidden_units // 256) * 128
    core = replicas.bit(0)
    pair_parts = []
    for low, high in ((0, cut), (cut, hidden_units)):
        gate_range, up_range = grad_gate[:, low:high], grad_up[:, low:high]
        got = replicas.swap_core(jnp.where(core == 0, up_range, gate_range))
        summed = added(jnp.where(core == 0, gate_range, up_range), got)
        summed = summed.reshape(group_size, eighth, rows_own // eighth, high - low)
        pair_parts.append(summed.transpose(1, 0, 2, 3))
    first, second = pair_parts
    down = replicas.first(down, far)
    out_own, out_other = token_product(
        out_part_kernel, (activ_low,), out_weights, width, kinds
    )
    if group.pair:
        norm_got = group.swap(norm_other)
    else:
        norm_own = group.own_tokens(jnp.concatenate([norm_own, norm_other]))
        norm_got = jnp.zeros((length, width), jnp.bfloat16)
    norm_own, norm_got, out_own, out_other, down, first, second = together(
        norm_own, norm_got, out_own, out_other, down, first, second
    )
    columns = full_qkv.shape[1] + width
    unit = 16 * eighth
    padded = -(-(rows_own + 16) // unit) * unit
    attn, input_grad = attention_backward(
        group_size, padded, early, late, norm_own, norm_got, cotangent, gain_mlp_row, full_output,
        query_rot, key_rot, value_low, segs_col, segs_row, cosine, sine, normed_low, full_qkv,
        tokens, gain_attn_row,
    )
    down = replicas.first(down, far[1:])
    first = replicas.first(first, near_first)
    second = replicas.first(second, far)
    if group.pair:
        out_sum = out_own + group.swap(out_other).astype(jnp.float32)
    else:
        out_sum = group.own_tokens(jnp.concatenate([out_own, out_other]))
    attn, down, first, second = together(attn, down, first, second)
    output = (middle + live * out_sum).astype(jnp.bfloat16)
    attn = replicas.scatter(
        attn.reshape(group_size, 2, padded // 2, columns).transpose(1, 0, 2, 3), 0
    )
    attn = group.sum_parts(attn).reshape(eighth, -1, columns)
    attn = replicas.scatter_all(attn, near_first)
    down = replicas.scatter_all(down, far[2:])
    first = group.exchange_parts(replicas.scatter_all(first, near_first[1:]))
    second = group.exchange_parts(replicas.scatter_all(second, far[1:]))
    down = replicas.gather(replicas.gather_all(down, far), 0)
    first = replicas.gather_all(first, near_first)
    second = replicas.gather_all(second, far)
    attn = replicas.gather_all(attn, near_first)
    shard_down = down.reshape(-1, width).astype(jnp.float32)
    gate_parts = [[] for _ in range(group_size)]
    up_parts = [[] for _ in range(group_size)]
    for mine in (first, second):
        got = replicas.swap_core(mine)
        for matrix, parts in (
            (jnp.where(core == 0, mine, got), gate_parts),
            (jnp.where(core == 0, got, mine), up_parts),
        ):
            for sender in range(group_size):
                parts[sender].append(matrix[:, sender].reshape(rows_own, -1))
    shard_gate, shard_up = (
        jnp.concatenate(sum(parts, []), axis=1).astype(jnp.float32)
        for parts in (gate_parts, up_parts)
    )
    attn_sum = replicas.gather(attn, 0).reshape(padded, columns).astype(jnp.float32)
    shard_query = attn_sum[:rows_own, :qw]
    shard_key = attn_sum[:rows_own, qw : qw + kw]
    shard_value = attn_sum[:rows_own, qw + kw : qw + 2 * kw]
    shard_output = attn_sum[:rows_own, qw + 2 * kw :]
    bias_sum = attn_sum[rows_own, : columns - width]
    shard_vectors = tuple(
        chosen(vector.reshape(group_size, -1), group.at)
        for vector in (
            bias_sum[:qw],
            bias_sum[qw : qw + kw],
            bias_sum[qw + kw :],
            attn_sum[rows_own, columns - width :],
            attn_sum[rows_own + 1, :width],
        )
    )
    return (
        output,
        input_grad,
        shard_query,
        shard_key,
        shard_value,
        shard_output,
        shard_gate,
        shard_up,
        shard_down,
    ) + shard_vectors


def solution(mesh):
    placed = (
        P(("rep", "fsdp"), None),
        P(("rep", "fsdp")),
        P(("rep", "fsdp"), None),
        P("fsdp", None),
        P("fsdp", None),
        P("fsdp", None),
        P("fsdp", None),
        P("fsdp", None),
        P("fsdp", None),
        P("fsdp", None),
        P("fsdp"),
        P("fsdp"),
        P("fsdp"),
        P("fsdp"),
        P("fsdp"),
    )
    return jax.shard_map(
        functools.partial(
            shards, group_size=mesh.shape["fsdp"], replica_count=mesh.shape["rep"]
        ),
        mesh=mesh,
        in_specs=placed,
        out_specs=(
            P(("rep", "fsdp"), None),
            P(("rep", "fsdp"), None),
            P("fsdp", None),
            P("fsdp", None),
            P("fsdp", None),
            P("fsdp", None),
            P("fsdp", None),
            P("fsdp", None),
            P("fsdp", None),
            P("fsdp"),
            P("fsdp"),
            P("fsdp"),
            P("fsdp"),
            P("fsdp"),
        ),
        check_vma=False,
    )
```

```python
import functools

import jax
import jax.numpy as jnp
from jax import lax
from jax.experimental import pallas as pl
from jax.experimental.pallas import tpu as pltpu
from jax.sharding import PartitionSpec as P

HEAD_DIM = 64


EPSILON = 1e-06
THETA = 1000000.0
NEGATIVE = -1e30


def positions(segs):
    length = segs.shape[0]
    index = jnp.arange(length, dtype=jnp.int32)
    before = jnp.concatenate([jnp.full((1,), -2, dtype=jnp.int32), segs[:-1]])
    starts = lax.cummax(jnp.where(segs != before, index, jnp.zeros_like(index)), axis=0)
    return (index - starts).astype(jnp.float32)


def rope_tables(segs, head_dim):
    halfway = head_dim // 2
    inverse = THETA ** (-(jnp.arange(halfway, dtype=jnp.float32) * 2.0 / head_dim))
    angles = positions(segs)[:, None] * inverse[None, :]
    return (jnp.cos(angles), jnp.sin(angles))


def normed(values, gain):
    scale = lax.rsqrt(jnp.mean(values * values, axis=-1, keepdims=True) + EPSILON)
    return values * scale * gain


def forward_product(left, right):
    return jnp.dot(left, right, preferred_element_type=jnp.float32)


def contract_rows(left, right):
    return lax.dot_general(
        left, right, (((0,), (0,)), ((), ())), preferred_element_type=jnp.float32
    )


def contract_cols(left, right):
    return lax.dot_general(
        left, right, (((1,), (1,)), ((), ())), preferred_element_type=jnp.float32
    )


LANES = 128


def lane_index(shape):
    return lax.broadcasted_iota(jnp.int32, shape, len(shape) - 1)


def swapped_halves(values):
    half = HEAD_DIM // 2
    lanes = lane_index(values.shape)
    return jnp.where(
        lanes % HEAD_DIM < half,
        pltpu.roll(values, LANES - half, 1),
        pltpu.roll(values, half, 1),
    )


def doubled(pair, head):
    lanes = lane_index(pair.shape)
    wide = pair.astype(jnp.float32)
    other = pltpu.roll(wide, HEAD_DIM, 1)
    return jnp.where((lanes < HEAD_DIM) == (head == 0), wide, other).astype(jnp.bfloat16)


def one_head(pair, parity):
    lanes = lane_index(pair.shape)
    return jnp.where((lanes < HEAD_DIM) == (parity == 0), pair, jnp.zeros_like(pair))


def mask_bias(key_segs, row_segs, row_start):
    keys, rows = key_segs.shape[0], row_segs.shape[1]
    key_index = lax.broadcasted_iota(jnp.int32, (keys, rows), 0)
    row_index = row_start + lax.broadcasted_iota(jnp.int32, (keys, rows), 1)
    allowed = (key_segs == row_segs) & (row_index >= key_index)
    return jnp.where(allowed, 0.0, NEGATIVE).astype(jnp.float32)


def is_live(segs):
    return jnp.where(segs >= 0, 1.0, 0.0)


def turned_over(values):
    return jnp.transpose(values.astype(jnp.float32)).astype(jnp.bfloat16)


def one_of_pair(first, second):
    rows = lax.broadcasted_iota(jnp.int32, first.shape, 0)
    return jnp.where(rows < HEAD_DIM, first, second)


def attend_rows(
    row_start, key_count, groups, pairs, segs_col, segs_row, query_rot, key_rot, value_low,
    bias, keys_two, values_over, attended, logs, tokens, w_output, gain, middle, mid_low,
):
    rows = attended.shape[0]
    for kv_head in range(2):
        keys_two[kv_head] = doubled(key_rot[:key_count, :], kv_head)
        values_over[kv_head] = turned_over(doubled(value_low[:key_count, :], kv_head))
    bias[...] = mask_bias(
        segs_col[:key_count], segs_row[:, row_start : row_start + rows], row_start
    )

    def one_pair(pair, carry):
        cols = pl.ds(pl.multiple_of(pair * LANES, LANES), LANES)
        queries = query_rot[row_start : row_start + rows, cols]
        results = []
        for parity in range(2):
            head = 2 * pair + parity
            kv_head = head // groups
            query = one_head(queries, parity) * jnp.asarray(HEAD_DIM**-0.5, jnp.bfloat16)
            scores = contract_cols(keys_two[kv_head], query) + bias[...]
            row_max = jnp.max(scores, axis=0, keepdims=True)
            exponent = jnp.exp(scores - row_max)
            row_total = jnp.sum(exponent, axis=0, keepdims=True)
            probs = (exponent * (1.0 / row_total)).astype(jnp.bfloat16)
            results.append(forward_product(values_over[kv_head], probs))
            logs[pl.ds(head, 1), :] = row_max + jnp.log(row_total)
        attended[:, cols] = jnp.transpose(one_of_pair(*results)).astype(jnp.bfloat16)
        return carry

    lax.fori_loop(0, pairs, one_pair, 0)
    mixed = forward_product(attended[...], w_output[...])
    here = slice(row_start, row_start + rows)
    total = tokens[here, :].astype(jnp.float32) + is_live(segs_col[here, :]) * mixed
    middle[...] = total
    mid_low[...] = normed(total, gain[...]).astype(jnp.bfloat16)


def early_kernel(
    groups, pairs, normed_low, w_qkv, bias_qkv, cosine, sine, segs_col, segs_row, tokens,
    w_output, gain, query_rot, key_rot, value_low, attended, logs, middle, mid_low,
    bias, keys_two, values_over,
):
    def project(pair):
        cols = pl.ds(pl.multiple_of(pair * LANES, LANES), LANES)
        return forward_product(normed_low[...], w_qkv[:, cols]) + bias_qkv[:, cols]

    def turned(values):
        return (values * cosine[...] + swapped_halves(values) * sine[...]).astype(jnp.bfloat16)

    def query_pair(pair, carry):
        cols = pl.ds(pl.multiple_of(pair * LANES, LANES), LANES)
        query_rot[:, cols] = turned(project(pair))
        return carry

    lax.fori_loop(0, pairs, query_pair, 0)
    key_rot[...] = turned(project(pairs))
    value_low[...] = project(pairs + 1).astype(jnp.bfloat16)
    attend_rows(
        0, attended.shape[0], groups, pairs, segs_col, segs_row, query_rot, key_rot, value_low,
        bias, keys_two, values_over, attended, logs, tokens, w_output, gain, middle, mid_low,
    )


def late_kernel(
    groups, pairs, query_rot, key_rot, value_low, segs_col, segs_row, tokens,
    w_output, gain, attended, logs, middle, mid_low, bias, keys_two, values_over,
):
    rows = attended.shape[0]
    attend_rows(
        rows, 2 * rows, groups, pairs, segs_col, segs_row, query_rot, key_rot, value_low,
        bias, keys_two, values_over, attended, logs, tokens, w_output, gain, middle, mid_low,
    )


def call(kernel, out_shape, scratch, cost, operands):
    return pl.pallas_call(
        kernel,
        out_shape=[jax.ShapeDtypeStruct(shape, kind) for shape, kind in out_shape],
        in_specs=[pl.BlockSpec(memory_space=pltpu.VMEM)] * len(operands),
        out_specs=[pl.BlockSpec(memory_space=pltpu.VMEM)] * len(out_shape),
        scratch_shapes=[pltpu.VMEM(shape, kind) for shape, kind in scratch],
        compiler_params=pltpu.CompilerParams(vmem_limit_bytes=56 * 2**20),
        cost_estimate=pl.CostEstimate(flops=cost, bytes_accessed=cost // 300, transcendentals=0),
    )(*operands)


def attention_shapes(length, key_count, w_output, kw):
    queries, width = w_output.shape
    rows = length // 2
    heads = -(-queries // HEAD_DIM // 8) * 8
    low, wide = jnp.bfloat16, jnp.float32
    half_out = [
        ((rows, queries), low), ((heads, rows), wide), ((rows, width), wide), ((rows, width), low)
    ]
    scratch = [
        ((key_count, rows), wide), ((2, key_count, LANES), low), ((2, LANES, key_count), low)
    ]
    return queries, queries // kw, queries // LANES, half_out, scratch


def attention_early(
    normed_low, w_qkv, bias_qkv, cosine, sine, segs_col, segs_row, tokens, w_output, gain
):
    length = tokens.shape[0]
    kw = (w_qkv.shape[1] - w_output.shape[0]) // 2
    queries, groups, pairs, half_out, scratch = attention_shapes(
        length, length // 2, w_output, kw
    )
    whole = [((length, columns), jnp.bfloat16) for columns in (queries, kw, kw)]
    query_rot, key_rot, value_low, *early = call(
        functools.partial(early_kernel, groups, pairs),
        whole + half_out,
        scratch,
        10**6,
        (normed_low, w_qkv, bias_qkv, cosine, sine, segs_col, segs_row, tokens, w_output, gain),
    )
    return query_rot, key_rot, value_low, early


def attention_late(query_rot, key_rot, value_low, segs_col, segs_row, tokens, w_output, gain):
    length = tokens.shape[0]
    _, groups, pairs, half_out, scratch = attention_shapes(
        length, length, w_output, key_rot.shape[1]
    )
    return call(
        functools.partial(late_kernel, groups, pairs),
        half_out,
        scratch,
        10**6,
        (query_rot, key_rot, value_low, segs_col, segs_row, tokens, w_output, gain),
    )


def norm_pull(values, gain, grad):
    scale = lax.rsqrt(jnp.mean(values * values, axis=-1, keepdims=True) + EPSILON)
    unit = values * scale
    inner = grad * gain
    pull = scale * (inner - unit * jnp.mean(inner * unit, axis=-1, keepdims=True))
    return pull, jnp.sum(grad * unit, axis=0, keepdims=True)


def backward_kernel(
    groups, pairs, devices, mid_early, mid_late, norm_own, norm_got, cotangent, gain_mlp, w_output,
    att_early, att_late, log_early, log_late, query_rot, key_rot, value_low, segs_col, segs_row,
    cosine, sine, normed_low, w_qkv, tokens, gain_attn,
    sums, input_grad, attn_grad, attended_grad, low_grads, bias, keys_two, keys_over, values_two, key_grad, value_grad,
    qkv_sums, out_sums,
):
    rows = mid_early.shape[0]
    length = 2 * rows
    parts = ((0, mid_early, att_early, log_early), (rows, mid_late, att_late, log_late))
    width, columns = w_qkv.shape
    own = width // devices
    padded = sums.shape[0] // devices

    def sum_row(row, first, value):
        low = value.astype(jnp.bfloat16)
        for device in range(devices):
            at = device * padded + own + row
            sums[at : at + 1, first : first + low.shape[1]] = low

    for device in range(devices):
        at = device * padded + own
        sums[at : at + padded - own, :] = jnp.zeros((padded - own, sums.shape[1]), jnp.bfloat16)
    gain_sum = jnp.zeros(gain_mlp.shape, jnp.float32)
    for start, middle, _, _ in parts:
        here = slice(start, start + rows)
        pull, gain_part = norm_pull(
            middle[...],
            gain_mlp[...],
            norm_own[here, :] + norm_got[here, :].astype(jnp.float32),
        )
        gain_sum = gain_sum + gain_part
        total = cotangent[here, :].astype(jnp.float32) + pull
        input_grad[here, :] = total
        attn_grad[here, :] = (is_live(segs_col[here, :]) * total).astype(jnp.bfloat16)
        bias[: start + rows, here] = mask_bias(segs_col[: start + rows], segs_row[:, here], start)
    sum_row(1, 0, gain_sum)
    for kv_head in range(2):
        keys_two[kv_head] = doubled(key_rot[...], kv_head)
        keys_over[kv_head] = turned_over(keys_two[kv_head])
        values_two[kv_head] = doubled(value_low[...], kv_head)
    key_grad[...] = jnp.zeros_like(key_grad)
    value_grad[...] = jnp.zeros_like(value_grad)
    for start in range(0, length, rows):
        here = slice(start, start + rows)
        attended_grad[here, :] = contract_cols(attn_grad[here, :], w_output[...]).astype(
            jnp.bfloat16
        )

    def turned_back(values, here):
        return values * cosine[here, :] - swapped_halves(values) * sine[here, :]

    def one_pair(pair, carry):
        cols = pl.ds(pl.multiple_of(pair * LANES, LANES), LANES)
        out_grad = jnp.zeros((LANES, attn_grad.shape[1]), jnp.float32)
        for start, _, attended, logs in parts:
            here = slice(start, start + rows)
            keys = start + rows
            out_grad = out_grad + contract_rows(attended[:, cols], attn_grad[here, :])
            queries = query_rot[here, cols]
            grads = attended_grad[here, cols]
            results = []
            for parity in range(2):
                head = 2 * pair + parity
                kv_head = head // groups
                query = one_head(queries, parity) * jnp.asarray(HEAD_DIM**-0.5, jnp.bfloat16)
                grad = one_head(grads, parity)
                scores = contract_cols(keys_two[kv_head, :keys], query) + bias[:keys, here]
                probs = jnp.exp(scores - logs[pl.ds(head, 1), :])
                prob_grad = contract_cols(values_two[kv_head, :keys], grad)
                inner = jnp.sum(prob_grad * probs, axis=0, keepdims=True)
                score_grad = (probs * (prob_grad - inner)).astype(jnp.bfloat16)
                value_grad[kv_head, :keys] += forward_product(probs.astype(jnp.bfloat16), grad)
                key_grad[kv_head, :keys] += forward_product(score_grad, query)
                results.append(forward_product(keys_over[kv_head, :, :keys], score_grad))
            query_grad = jnp.transpose(one_of_pair(*results)) * HEAD_DIM**-0.5
            low = turned_back(query_grad, here).astype(jnp.bfloat16)
            low_grads[here, cols] = low
        out_sums[cols, :] = out_grad.astype(jnp.bfloat16)
        return carry

    lax.fori_loop(0, pairs, one_pair, 0)

    def folded(pair_sums):
        both = [pair_sums[at] + pltpu.roll(pair_sums[at], HEAD_DIM, 1) for at in range(2)]
        return jnp.where(lane_index(both[0].shape) < HEAD_DIM, both[0], both[1])

    everywhere = slice(0, length)
    key_low = turned_back(folded(key_grad), everywhere).astype(jnp.bfloat16)
    value_grad_low = folded(value_grad).astype(jnp.bfloat16)
    for at, low in ((pairs, key_low), (pairs + 1, value_grad_low)):
        cols = slice(at * LANES, (at + 1) * LANES)
        low_grads[:, cols] = low
    sum_row(0, 0, jnp.sum(low_grads[...].astype(jnp.float32), axis=0, keepdims=True))

    def weight_rows(block, carry):
        cols = pl.ds(pl.multiple_of(block * LANES, LANES), LANES)
        qkv_sums[cols, :] = contract_rows(normed_low[:, cols], low_grads[...]).astype(jnp.bfloat16)
        return carry

    lax.fori_loop(0, width // LANES, weight_rows, 0)
    for device in range(devices):
        here = slice(device * padded, device * padded + own)
        there = slice(device * own, (device + 1) * own)
        sums[here, :columns] = qkv_sums[there, :]
        sums[here, columns:] = out_sums[there, :]
    gain_sum = jnp.zeros(gain_attn.shape, jnp.float32)
    for start in range(0, length, rows):
        here = slice(start, start + rows)
        norm_in = contract_cols(low_grads[here, :], w_qkv[...])
        pull, gain_part = norm_pull(tokens[here, :].astype(jnp.float32), gain_attn[...], norm_in)
        gain_sum = gain_sum + gain_part
        input_grad[here, :] += pull
    sum_row(0, columns, gain_sum)


def attention_backward(
    devices, padded, early, late, norm_own, norm_got, cotangent, gain_mlp, w_output, query_rot, key_rot, value_low,
    segs_col, segs_row, cosine, sine, normed_low, w_qkv, tokens, gain_attn,
):
    length, width = tokens.shape
    queries = w_output.shape[0]
    columns = w_qkv.shape[1]
    kw = (columns - queries) // 2
    low, wide = jnp.bfloat16, jnp.float32
    return call(
        functools.partial(backward_kernel, queries // kw, queries // LANES, devices),
        [((devices * padded, columns + width), low), ((length, width), wide)],
        [
            ((length, width), low),
            ((length, queries), low),
            ((length, columns), low),
            ((length, length), wide),
            ((2, length, LANES), low),
            ((2, LANES, length), low),
            ((2, length, LANES), low),
            ((2, length, LANES), wide),
            ((2, length, LANES), wide),
            ((width, columns), low),
            ((queries, width), low),
        ],
        10**6,
        (early[2], late[2], norm_own, norm_got, cotangent, gain_mlp, w_output, early[0], late[0],
         early[1], late[1], query_rot, key_rot, value_low, segs_col, segs_row, cosine, sine,
         normed_low, w_qkv, tokens, gain_attn),
    )


def swapped(value, axis, bit, size):
    step = 1 << bit
    return lax.ppermute(value, axis, [(at, at ^ step) for at in range(size)])


def chosen(parts, at):
    return lax.dynamic_index_in_dim(parts, at, 0, keepdims=False)


def added(left, right):
    return (left.astype(jnp.float32) + right.astype(jnp.float32)).astype(jnp.bfloat16)


def ordered(own, other, bit):
    return jnp.where(bit == 0, jnp.stack([own, other]), jnp.stack([other, own]))


def hidden_kernel(carries, mid_low, mlp_grad, w_gate, w_up, w_down, *refs):
    activ, gate_grad, up_grad = refs[carries:]
    gate = forward_product(mid_low[...], w_gate[...])
    upward = forward_product(mid_low[...], w_up[...])
    grad = contract_cols(mlp_grad[...], w_down[...])
    sigmoid = jax.nn.sigmoid(gate)
    silu = gate * sigmoid
    activ[...] = (silu * upward).astype(jnp.bfloat16)
    gate_grad[...] = (grad * upward * (sigmoid + silu * (1.0 - sigmoid))).astype(jnp.bfloat16)
    up_grad[...] = (grad * silu).astype(jnp.bfloat16)


def whole_block(array):
    return pl.BlockSpec(array.shape, lambda at: (0,) * array.ndim)


def row_block(array, rows, start=0):
    return pl.BlockSpec((rows, array.shape[1]), lambda at: (at + start, 0))


def grid_call(kernel, grid, operands, in_specs, out_shape, out_specs, flops, aliases=None):
    return pl.pallas_call(
        kernel,
        grid=grid,
        out_shape=out_shape,
        in_specs=in_specs,
        out_specs=out_specs,
        input_output_aliases=aliases or {},
        compiler_params=pltpu.CompilerParams(vmem_limit_bytes=56 * 2**20),
        cost_estimate=pl.CostEstimate(flops=flops, bytes_accessed=10**3, transcendentals=0),
    )(*operands)


def hidden_part(mid_low, mlp_grad, w_gate, w_up, w_down, total, start, carried):
    rows, columns = 512, 4 * LANES
    width, hidden = w_gate.shape
    first = start // rows
    shapes = [jax.ShapeDtypeStruct((total, hidden), jnp.bfloat16)] * 3
    tokens = pl.BlockSpec((rows, width), lambda token, unit: (token, 0))
    across = pl.BlockSpec((width, columns), lambda token, unit: (0, unit))
    return grid_call(
        functools.partial(hidden_kernel, len(carried)),
        (mid_low.shape[0] // rows, pl.cdiv(hidden, columns)),
        [mid_low, mlp_grad, w_gate, w_up, w_down] + list(carried),
        [tokens, tokens, across, across]
        + [pl.BlockSpec((columns, width), lambda token, unit: (unit, 0))]
        + [pl.BlockSpec(memory_space=pl.ANY)] * len(carried),
        shapes,
        [pl.BlockSpec((rows, columns), lambda token, unit: (token + first, unit))] * 3,
        10**6,
        {5 + at: at for at in range(len(carried))},
    )


def norm_part_kernel(gate_grad, up_grad, w_gate, w_up, first, second):
    value = contract_cols(gate_grad[...], w_gate[...]) + contract_cols(up_grad[...], w_up[...])
    two_parts(value, first, second)


def out_part_kernel(activ, w_down, first, second):
    two_parts(forward_product(activ[...], w_down[...]), first, second)


def two_parts(value, first, second):
    at, half = pl.program_id(0), pl.num_programs(0) // 2

    @pl.when(at < half)
    def _():
        first[...] = value.astype(first.dtype)

    @pl.when(at >= half)
    def _():
        second[...] = value.astype(second.dtype)


def token_product(kernel, activs, weights, width, kinds):
    rows = 256
    total, hidden = activs[0].shape
    half = total // rows // 2
    return grid_call(
        kernel,
        (2 * half,),
        list(activs) + list(weights),
        [row_block(activ, rows) for activ in activs] + [whole_block(weight) for weight in weights],
        [jax.ShapeDtypeStruct((total // 2, width), kind) for kind in kinds],
        [
            pl.BlockSpec((rows, width), lambda at: (jnp.minimum(at, half - 1), 0)),
            pl.BlockSpec((rows, width), lambda at: (jnp.maximum(at - half, 0), 0)),
        ],
        10**6,
    )


def together(*values):
    return lax.optimization_barrier(values)


class Group:
    def __init__(self, size, replicas):
        self.size = size
        self.replicas = replicas
        self.at = lax.axis_index("fsdp")
        self.replica = lax.axis_index("rep")
        self.pair = size == 2 and replicas % 2 == 0

    def swap(self, value):
        return swapped(value, "fsdp", 0, 2)

    def fetched(self, rows, bits):
        start, count = 0, rows.shape[0]
        for bit in bits:
            count //= 2
            start = start + ((self.replica >> bit) & 1) * count
        return self.swap(lax.dynamic_slice_in_dim(rows, start, count, 0))

    def shared(self, part, bits):
        for bit in reversed(bits):
            other = swapped(part, "rep", bit, self.replicas)
            part = ordered(part, other, (self.replica >> bit) & 1)
            part = part.reshape((-1,) + part.shape[2:])
        return part

    def joined(self, own, other):
        return ordered(own, other, self.at).reshape((-1,) + own.shape[1:])

    def whole_vector(self, vector):
        if not self.pair:
            return lax.all_gather(vector, "fsdp", axis=0, tiled=False)
        return ordered(vector, self.swap(vector), self.at)

    def columns(self, rows, owner):
        width = rows.shape[1] // 2
        return lax.dynamic_slice_in_dim(rows, owner * width, width, 1)

    def plain_weights(self, qkv, w_output, w_gate, w_up):
        return (
            lax.all_gather(qkv, "fsdp", axis=0, tiled=True),
            lax.all_gather(w_output, "fsdp", axis=0, tiled=True),
            lax.all_to_all(w_gate, "fsdp", 1, 0, tiled=True),
            lax.all_to_all(w_up, "fsdp", 1, 0, tiled=True),
        )

    def all_tokens(self, value):
        return lax.all_gather(value, "fsdp", axis=0, tiled=True)

    def own_tokens(self, partial):
        return lax.psum_scatter(partial, "fsdp", scatter_dimension=0, tiled=True)

    def sum_parts(self, parts):
        if not self.pair:
            return lax.psum_scatter(parts, "fsdp", scatter_dimension=0, tiled=False)
        got = self.swap(chosen(parts, 1 - self.at))
        return added(chosen(parts, self.at), got)

    def exchange_parts(self, parts):
        if not self.pair:
            return lax.all_to_all(parts, "fsdp", 0, 0, tiled=True)
        got = self.swap(chosen(parts, 1 - self.at))
        return ordered(chosen(parts, self.at), got, self.at)


class Replicas:
    def __init__(self, size):
        self.size = size
        self.at = lax.axis_index("rep")
        self.bits = size.bit_length() - 1
        self.far = list(range(1, self.bits))

    def bit(self, bit):
        return (self.at >> bit) & 1

    def swap_core(self, value):
        return swapped(value, "rep", 0, self.size)

    def scatter(self, parts, bit):
        mine = self.bit(bit)
        got = swapped(chosen(parts, 1 - mine), "rep", bit, self.size)
        return added(chosen(parts, mine), got)

    def gather(self, value, bit):
        return ordered(value, swapped(value, "rep", bit, self.size), self.bit(bit))

    def first(self, parts, order):
        if not order:
            return parts
        return self.scatter(parts.reshape((2, -1) + parts.shape[1:]), order[0])

    def scatter_all(self, parts, order):
        for at in range(len(order)):
            parts = self.first(parts, order[at:])
        return parts.reshape(parts.shape[1:])

    def gather_all(self, value, order):
        value = value[None]
        for bit in reversed(order):
            value = self.gather(value, bit)
            value = value.reshape((value.shape[0] * value.shape[1],) + value.shape[2:])
        return value


def shards(
    tokens,
    segments,
    cotangent,
    w_query,
    w_key,
    w_value,
    w_output,
    w_gate,
    w_up,
    w_down,
    b_query,
    b_key,
    b_value,
    gain_attn,
    gain_mlp,
    group_size,
    replica_count,
):
    group = Group(group_size, replica_count)
    replicas = Replicas(replica_count)
    far = replicas.far
    near_first = [far[1], far[0]] + far[2:]
    eighth = 1 << len(far)
    width = tokens.shape[1]
    rows_own = w_query.shape[0]
    qw, kw = w_query.shape[1], w_key.shape[1]
    vectors = group.whole_vector(
        jnp.concatenate([b_query, b_key, b_value, gain_attn, gain_mlp])
    ).astype(jnp.float32)
    cuts = [0]
    for part in (b_query, b_key, b_value, gain_attn, gain_mlp):
        cuts.append(cuts[-1] + part.shape[0])
    bias_query, bias_key, bias_value, full_gain_attn, full_gain_mlp = (
        vectors[:, low:high].reshape(-1) for low, high in zip(cuts[:-1], cuts[1:])
    )
    qkv = jnp.concatenate([w_query, w_key, w_value], axis=1)
    live = (segments >= 0).astype(jnp.float32)[:, None]
    mlp_grad = (live * cotangent.astype(jnp.float32)).astype(jnp.bfloat16)
    cosine, sine = rope_tables(segments, HEAD_DIM)
    copies = LANES // HEAD_DIM
    cosine = jnp.concatenate([cosine, cosine] * copies, axis=1)
    sine = jnp.concatenate([-sine, sine] * copies, axis=1)
    segs_col, segs_row = segments[:, None], segments[None, :]
    normed_low = normed(tokens.astype(jnp.float32), full_gain_attn).astype(jnp.bfloat16)
    gain_attn_row, gain_mlp_row = full_gain_attn[None, :], full_gain_mlp[None, :]
    bias_row = jnp.concatenate([bias_query, bias_key, bias_value])[None, :]
    if group.pair:
        cores = [0]
        chips = [0, 1] if replica_count % 4 == 0 else [0]
        got_qkv, got_output = group.fetched(qkv, cores), group.fetched(w_output, cores)
        got_qkv, got_output, w_gate, w_up = together(got_qkv, got_output, w_gate, w_up)
        full_qkv = group.joined(qkv, group.shared(got_qkv, cores))
        full_output = group.joined(w_output, group.shared(got_output, cores))
        got_gate = group.fetched(group.columns(w_gate, 1 - group.at), chips)
        got_up = group.fetched(group.columns(w_up, 1 - group.at), cores)
    else:
        full_qkv, full_output, part_gate, part_up = group.plain_weights(
            qkv, w_output, w_gate, w_up
        )
    query_rot, key_rot, value_low, early = attention_early(
        normed_low, full_qkv, bias_row, cosine, sine, segs_col, segs_row, tokens, full_output,
        gain_mlp_row,
    )
    if group.pair:
        query_rot, early, got_gate, mlp_grad = together(query_rot, early, got_gate, mlp_grad)
        got_gate = group.shared(got_gate, chips[1:])
        others = [group.swap(early[3])]
        mlp_other = group.swap(mlp_grad)
    late = attention_late(
        query_rot, key_rot, value_low, segs_col, segs_row, tokens, full_output, gain_mlp_row
    )
    mid_own = jnp.concatenate([early[3], late[3]])
    length = tokens.shape[0]
    if group.pair:
        late, got_gate, got_up, others = together(late, got_gate, got_up, others)
        others.append(group.swap(late[3]))
        got_gate, got_up = group.shared(got_gate, cores), group.shared(got_up, cores)
        part_gate = group.joined(group.columns(w_gate, group.at), got_gate)
        part_up = group.joined(group.columns(w_up, group.at), got_up)
        hidden = hidden_part(
            mid_own, mlp_grad, part_gate, part_up, w_down, group_size * length, 0, ()
        )
        hidden, others, mlp_other = together(hidden, others, mlp_other)
        mid_other = jnp.concatenate(others)
        activ_low, gate_grad, up_grad = hidden_part(
            mid_other, mlp_other, part_gate, part_up, w_down, group_size * length, length, hidden
        )
        mid_all = jnp.concatenate([mid_own, mid_other])
        mlp_grad_all = jnp.concatenate([mlp_grad, mlp_other])
    else:
        mid_all = group.all_tokens(mid_own)
        mlp_grad_all = group.all_tokens(mlp_grad)
        activ_low, gate_grad, up_grad = hidden_part(
            mid_all, mlp_grad_all, part_gate, part_up, w_down, group_size * length, 0, ()
        )
    middle = jnp.concatenate([early[2], late[2]])

    back_weights, out_weights = (part_gate, part_up), (w_down,)
    back = (gate_grad, up_grad)
    kinds = (jnp.float32, jnp.bfloat16) if group.pair else (jnp.float32, jnp.float32)
    norm_own, norm_other = token_product(norm_part_kernel, back, back_weights, width, kinds)
    norm_own, norm_other, activ_low, back = together(norm_own, norm_other, activ_low, back)
    grad_down = contract_rows(activ_low, mlp_grad_all).astype(jnp.bfloat16)
    grad_down, back = together(grad_down, back)
    gate_grad, up_grad = back
    grad_gate = contract_rows(mid_all, gate_grad).astype(jnp.bfloat16)
    grad_up = contract_rows(mid_all, up_grad).astype(jnp.bfloat16)
    down = replicas.scatter(grad_down.reshape(2, -1, width), 0).reshape(eighth, -1, width)
    grad_gate, grad_up, down, back, activ_low = together(
        grad_gate, grad_up, down, back, activ_low
    )
    hidden_units = grad_gate.shape[1]
    cut = -(-hidden_units // 256) * 128
    core = replicas.bit(0)
    pair_parts = []
    for low, high in ((0, cut), (cut, hidden_units)):
        gate_range, up_range = grad_gate[:, low:high], grad_up[:, low:high]
        got = replicas.swap_core(jnp.where(core == 0, up_range, gate_range))
        summed = added(jnp.where(core == 0, gate_range, up_range), got)
        summed = summed.reshape(group_size, eighth, rows_own // eighth, high - low)
        pair_parts.append(summed.transpose(1, 0, 2, 3))
    first, second = pair_parts
    down = replicas.first(down, far)
    out_own, out_other = token_product(
        out_part_kernel, (activ_low,), out_weights, width, kinds
    )
    if group.pair:
        norm_got = group.swap(norm_other)
    else:
        norm_own = group.own_tokens(jnp.concatenate([norm_own, norm_other]))
        norm_got = jnp.zeros((length, width), jnp.bfloat16)
    norm_own, norm_got, out_own, out_other, down, first, second = together(
        norm_own, norm_got, out_own, out_other, down, first, second
    )
    columns = full_qkv.shape[1] + width
    unit = 16 * eighth
    padded = -(-(rows_own + 16) // unit) * unit
    attn, input_grad = attention_backward(
        group_size, padded, early, late, norm_own, norm_got, cotangent, gain_mlp_row, full_output,
        query_rot, key_rot, value_low, segs_col, segs_row, cosine, sine, normed_low, full_qkv,
        tokens, gain_attn_row,
    )
    down = replicas.first(down, far[1:])
    first = replicas.first(first, near_first)
    second = replicas.first(second, far)
    if group.pair:
        out_sum = out_own + group.swap(out_other).astype(jnp.float32)
    else:
        out_sum = group.own_tokens(jnp.concatenate([out_own, out_other]))
    attn, down, first, second = together(attn, down, first, second)
    output = (middle + live * out_sum).astype(jnp.bfloat16)
    attn = replicas.scatter(
        attn.reshape(group_size, 2, padded // 2, columns).transpose(1, 0, 2, 3), 0
    )
    attn = group.sum_parts(attn).reshape(eighth, -1, columns)
    attn = replicas.scatter_all(attn, near_first)
    down = replicas.scatter_all(down, far[2:])
    first = group.exchange_parts(replicas.scatter_all(first, near_first[1:]))
    second = group.exchange_parts(replicas.scatter_all(second, far[1:]))
    down = replicas.gather(replicas.gather_all(down, far), 0)
    first = replicas.gather_all(first, near_first)
    second = replicas.gather_all(second, far)
    attn = replicas.gather_all(attn, near_first)
    shard_down = down.reshape(-1, width).astype(jnp.float32)
    gate_parts = [[] for _ in range(group_size)]
    up_parts = [[] for _ in range(group_size)]
    for mine in (first, second):
        got = replicas.swap_core(mine)
        for matrix, parts in (
            (jnp.where(core == 0, mine, got), gate_parts),
            (jnp.where(core == 0, got, mine), up_parts),
        ):
            for sender in range(group_size):
                parts[sender].append(matrix[:, sender].reshape(rows_own, -1))
    shard_gate, shard_up = (
        jnp.concatenate(sum(parts, []), axis=1).astype(jnp.float32)
        for parts in (gate_parts, up_parts)
    )
    attn_sum = replicas.gather(attn, 0).reshape(padded, columns).astype(jnp.float32)
    shard_query = attn_sum[:rows_own, :qw]
    shard_key = attn_sum[:rows_own, qw : qw + kw]
    shard_value = attn_sum[:rows_own, qw + kw : qw + 2 * kw]
    shard_output = attn_sum[:rows_own, qw + 2 * kw :]
    bias_sum = attn_sum[rows_own, : columns - width]
    shard_vectors = tuple(
        chosen(vector.reshape(group_size, -1), group.at)
        for vector in (
            bias_sum[:qw],
            bias_sum[qw : qw + kw],
            bias_sum[qw + kw :],
            attn_sum[rows_own, columns - width :],
            attn_sum[rows_own + 1, :width],
        )
    )
    return (
        output,
        input_grad,
        shard_query,
        shard_key,
        shard_value,
        shard_output,
        shard_gate,
        shard_up,
        shard_down,
    ) + shard_vectors


def solution(mesh):
    placed = (
        P(("rep", "fsdp"), None),
        P(("rep", "fsdp")),
        P(("rep", "fsdp"), None),
        P("fsdp", None),
        P("fsdp", None),
        P("fsdp", None),
        P("fsdp", None),
        P("fsdp", None),
        P("fsdp", None),
        P("fsdp", None),
        P("fsdp"),
        P("fsdp"),
        P("fsdp"),
        P("fsdp"),
        P("fsdp"),
    )
    return jax.shard_map(
        functools.partial(
            shards, group_size=mesh.shape["fsdp"], replica_count=mesh.shape["rep"]
        ),
        mesh=mesh,
        in_specs=placed,
        out_specs=(
            P(("rep", "fsdp"), None),
            P(("rep", "fsdp"), None),
            P("fsdp", None),
            P("fsdp", None),
            P("fsdp", None),
            P("fsdp", None),
            P("fsdp", None),
            P("fsdp", None),
            P("fsdp", None),
            P("fsdp"),
            P("fsdp"),
            P("fsdp"),
            P("fsdp"),
            P("fsdp"),
        ),
        check_vma=False,
    )
```
